256 devices in a mesh: orient: 16 (over y_lo, x, core), dom: 16 (over y_hi, z).
Axes of the slice: x: 4, y: 4 (y_hi: 2, y_lo: 2; y = y_hi * 2 + y_lo), z: 8, core: 2. Of those that a mesh axis runs over, the one named last changes fastest.
Arguments:
- images: bfloat16 [1536, 32768], P('dom'), may hold values from -256 to 256
- shifts: int32 [1536, 2], P('dom'), may hold values from -8 to 8
- slices: bfloat16 [4096, 32768], P('orient', 'dom'), may hold values from -1 to 1
- class_of: int32 [4096], P('orient'), may hold values from 0 to 7
- log_prior: float32 [8], replicated, may hold values from -3 to 0
Outputs:
- backprojected: float32 [4096, 32768], P('orient', 'dom')
- log_norm: float32 [1536], P('dom')
The draws below stay inside these ranges and needn't reach their ends.
All inputs are finite; a program needn't handle non-finite values.
Results may differ from the reference program's by a relative error of at most 0.011.
Values may be sent and summed in bfloat16 or wider, within the bound.
No kernel may reach another device: no remote copies, remote signals or barrier semaphores. Data moves between devices by JAX's collectives and lax.ppermute only.
A program may use at most 128 MiB of HBM per device.

```python
import math
import jax
import jax.numpy as jnp

NPIX = 16384
BOX = 256
CLASSES = 8
SHIFT = 8
NORI = 4096
NIMG = 1536


def shift_table(key):
    return jax.random.randint(jax.random.fold_in(key, 5), (NIMG, 2), -SHIFT, SHIFT + 1).astype(jnp.int32)


def slice_table(key):
    base = jax.random.fold_in(key, 11)
    key_noise, key_scale = jax.random.split(base)
    noise = jax.random.truncated_normal(key_noise, -4.0, 4.0, (NORI, 2 * NPIX), jnp.float32) / math.sqrt(2 * NPIX)
    row_scale = jnp.exp(jax.random.uniform(key_scale, (NORI, 1), jnp.float32, math.log(0.4), math.log(4.0)))
    drawn = (noise * row_scale).reshape(NORI // 2, 2, 2 * NPIX)
    first = drawn[:, 0]
    second = drawn[:, 1]
    table = jnp.stack([first, second], axis=1).reshape(NORI, 2 * NPIX)
    return table


def draw_shifts(key, part):
    return shift_table(key)


def draw_slices(key, part):
    table = slice_table(key)
    return table.astype(jnp.bfloat16)


def draw_images(key, part):
    base = jax.random.fold_in(key, 3)
    key_noise, key_scale = jax.random.split(base)
    noise = jax.random.truncated_normal(key_noise, -4.0, 4.0, (NIMG, 2 * NPIX), jnp.float32)
    row_scale = jnp.exp(jax.random.uniform(key_scale, (NIMG, 1), jnp.float32, math.log(0.4), math.log(4.0)))
    drawn = noise * row_scale
    return drawn.astype(jnp.bfloat16)


def touch_ends(array, rng, smallest, high):
    longest = array.shape.index(max(array.shape))
    spots = []
    for shift in (0, 1):
        where = [jax.random.randint(jax.random.fold_in(rng, axis), (), 0, length) for axis, length in enumerate(array.shape)]
        where[longest] = (where[longest] + shift) % array.shape[longest]
        spots.append(tuple(where))
    return array.at[spots[0]].set(smallest).at[spots[1]].set(high)


def setup_inputs(seed: int = 0) -> dict:
    seeds = jax.random.split(jax.random.key(seed), 6)
    images = draw_images(jax.random.fold_in(seeds[5], 71), 0)
    shifts = draw_shifts(jax.random.fold_in(seeds[5], 71), 0)
    slices = draw_slices(jax.random.fold_in(seeds[5], 71), 0)
    class_of = touch_ends(jax.random.randint(seeds[3], (NORI,), 0, CLASSES), jax.random.fold_in(seeds[3], 1), 0, CLASSES - 1).astype(jnp.int32)
    log_prior = jnp.clip(jax.random.uniform(seeds[4], (CLASSES,), jnp.float32, -3.0, 0.0), -3.0, 0.0)
    return {"images": images, "shifts": shifts, "slices": slices, "class_of": class_of, "log_prior": log_prior}


def shift_images(images, shifts):
    coeff = jnp.arange(NPIX, dtype=jnp.int32)
    freq_x = coeff % 128
    freq_y = coeff // 128 - NPIX // 256
    turn = (freq_x[None, :] * shifts[:, 0:1] + freq_y[None, :] * shifts[:, 1:2]) % BOX
    angle = turn.astype(jnp.float32) * (2.0 * math.pi / BOX)
    cosine = jnp.cos(angle)
    sine = jnp.sin(angle)
    real_part = images[:, :NPIX].astype(jnp.float32)
    imag_part = images[:, NPIX:].astype(jnp.float32)
    new_real = real_part * cosine + imag_part * sine
    new_imag = imag_part * cosine - real_part * sine
    return jnp.concatenate([new_real, new_imag], axis=1).astype(jnp.bfloat16)


def reference(images, shifts, slices, class_of, log_prior):
    shifted = shift_images(images, shifts)
    prior = log_prior[class_of]
    slice_float = slices.astype(jnp.float32)
    norms = jnp.sum(slice_float * slice_float, axis=1)
    score = jnp.dot(shifted, slices.T, preferred_element_type=jnp.float32) - 0.5 * norms[None, :] + prior[None, :]
    peak = jnp.max(score, axis=1)
    total = jnp.sum(jnp.exp(score - peak[:, None]), axis=1)
    log_norm = peak + jnp.log(total)
    weights = (jnp.exp(score - peak[:, None]) / total[:, None]).astype(jnp.bfloat16)
    backprojected = jnp.dot(weights.T, shifted, preferred_element_type=jnp.float32)
    return backprojected, log_norm
```

```python
import functools
import math

import jax
import jax.numpy as jnp
from jax import lax
from jax.experimental import pallas as pl
from jax.experimental.pallas import tpu as pltpu
from jax.sharding import PartitionSpec as P

BOX = 256
LANES = 128
MIB = 1 << 20


def shift_kernel(parts, first, shifts, real, imag, out, cos_x, sin_x, cos_y, sin_y):
    step = pl.program_id(0)
    rows = real.shape[0]

    @pl.when(step == 0)
    def _():
        lane = lax.broadcasted_iota(jnp.int32, (rows, LANES), 1)
        turn_x = (lane * shifts[:, 0:1]) & (BOX - 1)
        turn_y = ((lane * parts + first[0] - first[1]) * shifts[:, 1:2]) & (BOX - 1)
        angle_x = turn_x.astype(jnp.float32) * (2.0 * math.pi / BOX)
        angle_y = turn_y.astype(jnp.float32) * (2.0 * math.pi / BOX)
        cos_x[...] = jnp.cos(angle_x)
        sin_x[...] = jnp.sin(angle_x)
        cos_y[...] = jnp.cos(angle_y)
        sin_y[...] = jnp.sin(angle_y)

    lane = lax.broadcasted_iota(jnp.int32, (rows, LANES), 1)
    cy = jnp.sum(jnp.where(lane == step, cos_y[...], 0.0), axis=1, keepdims=True)
    sy = jnp.sum(jnp.where(lane == step, sin_y[...], 0.0), axis=1, keepdims=True)
    cx = cos_x[...]
    sx = sin_x[...]
    cosine = cx * cy - sx * sy
    sine = sx * cy + cx * sy
    re = real[...].astype(jnp.float32)
    im = imag[...].astype(jnp.float32)
    out[0, 0] = (re * cosine + im * sine).astype(jnp.bfloat16)
    out[1, 0] = (im * cosine - re * sine).astype(jnp.bfloat16)


def shift_part(images, shifts, index, doms, parts):
    rows, width = images.shape
    half = doms // 2
    first = jnp.stack([index, jnp.int32(width // 2 // 256)]).astype(jnp.int32)
    out = pl.pallas_call(
        functools.partial(shift_kernel, parts),
        out_shape=jax.ShapeDtypeStruct((2, half, rows, LANES), jnp.bfloat16),
        grid_spec=pltpu.PrefetchScalarGridSpec(
            num_scalar_prefetch=1,
            grid=(half,),
            in_specs=[
                pl.BlockSpec((rows, 2), lambda i, first: (0, 0)),
                pl.BlockSpec((rows, LANES), lambda i, first: (0, i * parts + first[0])),
                pl.BlockSpec((rows, LANES), lambda i, first: (0, (i + half) * parts + first[0])),
            ],
            out_specs=pl.BlockSpec((2, 1, rows, LANES), lambda i, first: (0, i, 0, 0)),
            scratch_shapes=[pltpu.VMEM((rows, LANES), jnp.float32)] * 4,
        ),
        name="shift",
    )(first, shifts, images, images)
    return out.reshape(doms, rows, LANES)


def score_kernel(columns, slices, bias, out):
    block = jnp.concatenate([columns[p] for p in range(columns.shape[0])], axis=1)
    product = lax.dot_general(block, slices[...], (((1,), (1,)), ((), ())), preferred_element_type=jnp.float32)
    out[...] = product + bias[...]


def partial_score(columns, slices, bias, steps=4):
    parts, images, lanes = columns.shape
    rows = images // steps
    oris = slices.shape[0]
    return pl.pallas_call(
        score_kernel,
        out_shape=jax.ShapeDtypeStruct((images, oris), jnp.float32),
        grid=(steps,),
        in_specs=[
            pl.BlockSpec((parts, rows, lanes), lambda i: (0, i, 0)),
            pl.BlockSpec(slices.shape, lambda i: (0, 0)),
            pl.BlockSpec((1, oris), lambda i: (0, 0)),
        ],
        out_specs=pl.BlockSpec((rows, oris), lambda i: (i, 0)),
        compiler_params=pltpu.CompilerParams(vmem_limit_bytes=32 * MIB),
        name="score",
    )(columns, slices, bias)


def to_row(column):
    rows = column.shape[0]
    wide = jnp.broadcast_to(column, (rows, LANES))
    square = jnp.concatenate([wide, jnp.zeros((LANES - rows, LANES), jnp.float32)], axis=0)
    return jnp.transpose(square)[0:1]


def to_column(row, rows):
    return jnp.transpose(jnp.broadcast_to(row, (LANES, LANES)))[:rows, 0:1]


def total_kernel(pieces, score, stats):
    total = pieces[0]
    for d in range(1, pieces.shape[0]):
        total = total + pieces[d]
    score[...] = total
    peak = jnp.max(total, axis=1, keepdims=True)
    mass = jnp.sum(jnp.exp(total - peak), axis=1, keepdims=True)
    both = jnp.concatenate([to_row(peak), to_row(mass), jnp.zeros((6, LANES), jnp.float32)], axis=0)
    stats[...] = jnp.broadcast_to(both[None], stats.shape)


def total_score(pieces, parts):
    doms, rows, oris = pieces.shape
    return pl.pallas_call(
        total_kernel,
        out_shape=(
            jax.ShapeDtypeStruct((rows, oris), jnp.float32),
            jax.ShapeDtypeStruct((parts, 8, LANES), jnp.float32),
        ),
        compiler_params=pltpu.CompilerParams(vmem_limit_bytes=32 * MIB),
        name="total",
    )(pieces)


def weight_kernel(score, stats, weights, log_norm):
    rows = score.shape[0]
    peaks = stats[:, 0, :]
    masses = stats[:, 1, :]
    peak = jnp.max(peaks, axis=0, keepdims=True)
    total = jnp.sum(masses * jnp.exp(peaks - peak), axis=0, keepdims=True)
    used = lax.broadcasted_iota(jnp.int32, total.shape, 1) < rows
    total = jnp.where(used, total, 1.0)
    log_norm[...] = peak + jnp.log(total)
    chosen = jnp.exp(score[...] - to_column(peak, rows)) / to_column(total, rows)
    weights[...] = jnp.broadcast_to(chosen.astype(jnp.bfloat16)[None], weights.shape)


def weigh(score, stats, doms):
    rows, oris = score.shape
    return pl.pallas_call(
        weight_kernel,
        out_shape=(
            jax.ShapeDtypeStruct((doms, rows, oris), jnp.bfloat16),
            jax.ShapeDtypeStruct((1, LANES), jnp.float32),
        ),
        compiler_params=pltpu.CompilerParams(vmem_limit_bytes=32 * MIB),
        name="weigh",
    )(score, stats)


def project_kernel(weights, columns, out):
    block = jnp.concatenate([columns[p] for p in range(columns.shape[0])], axis=1)
    out[...] = lax.dot_general(
        weights[...], block, (((0,), (0,)), ((), ())), preferred_element_type=jnp.float32
    )


def project(weights, columns, steps=4):
    parts, images, lanes = columns.shape
    oris = weights.shape[1]
    take = parts // steps
    return pl.pallas_call(
        project_kernel,
        out_shape=jax.ShapeDtypeStruct((oris, parts * lanes), jnp.float32),
        grid=(steps,),
        in_specs=[
            pl.BlockSpec((images, oris), lambda i: (0, 0)),
            pl.BlockSpec((take, images, lanes), lambda i: (i, 0, 0)),
        ],
        out_specs=pl.BlockSpec((oris, take * lanes), lambda i: (0, i)),
        compiler_params=pltpu.CompilerParams(vmem_limit_bytes=32 * MIB),
        name="project",
    )(weights, columns)


def on_device(images, shifts, slices, class_of, log_prior, *, doms, parts):
    rows = images.shape[0]
    oris = slices.shape[0]
    own = shift_part(images, shifts, lax.axis_index("orient"), doms, parts)
    mine = lax.all_to_all(own, "dom", 0, 0).reshape(doms * rows, LANES)
    columns = lax.all_gather(mine, "orient")

    slice_float = slices.astype(jnp.float32)
    onehot = class_of[:, None] == jnp.arange(log_prior.shape[0], dtype=jnp.int32)[None, :]
    prior = jnp.sum(jnp.where(onehot, log_prior[None, :], 0.0), axis=1)
    bias = jnp.where(lax.axis_index("dom") == 0, prior, 0.0) - 0.5 * jnp.sum(slice_float * slice_float, axis=1)

    partial = partial_score(columns, slices, bias[None, :])
    pieces = lax.all_to_all(partial.reshape(doms, rows, oris), "dom", 0, 0)
    score, stats = total_score(pieces, parts)
    stats = lax.all_to_all(stats, "orient", 0, 0)
    copies, log_norm = weigh(score, stats, doms)
    weights = lax.all_to_all(copies, "dom", 0, 0).reshape(doms * rows, oris)
    return project(weights, columns), log_norm[0, :rows]


def solution(mesh):
    placed = (P("dom", None), P("dom", None), P("orient", "dom"), P("orient"), P())
    return jax.shard_map(
        functools.partial(on_device, doms=mesh.shape["dom"], parts=mesh.shape["orient"]),
        mesh=mesh,
        in_specs=placed,
        out_specs=(P("orient", "dom"), P("dom")),
        check_vma=False,
    )
```

```python
import functools
import math

import jax
import jax.numpy as jnp
from jax import lax
from jax.experimental import pallas as pl
from jax.experimental.pallas import tpu as pltpu
from jax.sharding import PartitionSpec as P

BOX = 256
LANES = 128
WIDE = 256
MIB = 1 << 20

ORI = 16
DOM = 16
RING = 4
HALF = DOM // 2
Z_GROUPS = [list(range(HALF)), list(range(HALF, DOM))]
CORE = [(i, i ^ 1) for i in range(ORI)]
Y_LOW = [(i, i ^ 8) for i in range(ORI)]
Y_HIGH = [(i, i ^ 8) for i in range(DOM)]


def along_x(by):
    return [(i, i // 8 * 8 + (i // 2 + by) % RING * 2 + i % 2) for i in range(ORI)]


def shift_kernel(place, shifts, real, imag, out, cos_x, sin_x, cos_y, sin_y):
    step = pl.program_id(0)
    rows = real.shape[0]
    lane = lax.broadcasted_iota(jnp.int32, (rows, LANES), 1)

    @pl.when(step == 0)
    def _():
        total = shifts.shape[1]
        image = lax.broadcasted_iota(jnp.int32, (rows, total), 0) + place[1] * rows
        own = image == lax.broadcasted_iota(jnp.int32, (rows, total), 1)
        by_x = jnp.sum(jnp.where(own, shifts[0:1, :], 0), axis=1, keepdims=True)
        by_y = jnp.sum(jnp.where(own, shifts[1:2, :], 0), axis=1, keepdims=True)
        freq_y = (lane // 2) * 16 + lane % 2 + 2 * place[0] - place[2]
        angle_x = ((lane * by_x) & (BOX - 1)).astype(jnp.float32) * (2.0 * math.pi / BOX)
        angle_y = ((freq_y * by_y) & (BOX - 1)).astype(jnp.float32) * (2.0 * math.pi / BOX)
        cos_x[...] = jnp.cos(angle_x)
        sin_x[...] = jnp.sin(angle_x)
        cos_y[...] = jnp.cos(angle_y)
        sin_y[...] = jnp.sin(angle_y)

    cx = cos_x[...]
    sx = sin_x[...]
    for part in range(2):
        pick = lane == 2 * step + part
        cy = jnp.sum(jnp.where(pick, cos_y[...], 0.0), axis=1, keepdims=True)
        sy = jnp.sum(jnp.where(pick, sin_y[...], 0.0), axis=1, keepdims=True)
        cosine = cx * cy - sx * sy
        sine = sx * cy + cx * sy
        here = slice(part * LANES, (part + 1) * LANES)
        re = real[:, here].astype(jnp.float32)
        im = imag[:, here].astype(jnp.float32)
        out[0, 0, :, here] = (re * cosine + im * sine).astype(jnp.bfloat16)
        out[0, 1, :, here] = (im * cosine - re * sine).astype(jnp.bfloat16)


def shift_part(images, shifts, share, core):
    rows, width = images.shape
    rows = rows // 2
    shares = width // DOM // WIDE
    place = jnp.stack([share, core, jnp.int32(width // 2 // 256)]).astype(jnp.int32)
    return pl.pallas_call(
        shift_kernel,
        out_shape=jax.ShapeDtypeStruct((HALF, 2, rows, WIDE), jnp.bfloat16),
        grid_spec=pltpu.PrefetchScalarGridSpec(
            num_scalar_prefetch=1,
            grid=(HALF,),
            in_specs=[
                pl.BlockSpec(shifts.shape, lambda i, place: (0, 0)),
                pl.BlockSpec((rows, WIDE), lambda i, place: (place[1], i * shares + place[0])),
                pl.BlockSpec((rows, WIDE), lambda i, place: (place[1], (i + HALF) * shares + place[0])),
            ],
            out_specs=pl.BlockSpec((1, 2, rows, WIDE), lambda i, place: (i, 0, 0, 0)),
            scratch_shapes=[pltpu.VMEM((rows, LANES), jnp.float32)] * 4,
        ),
        name="shift",
    )(place, shifts, images, images)


def gather_shares(own):
    send = lambda block, perm: lax.ppermute(block, "orient", perm)
    low = send(own, along_x(1))
    high = send(own, along_x(-1))
    across = send(own, Y_LOW)
    across_high = send(high, Y_LOW)
    across_low = send(across, along_x(1))
    far = send(high, along_x(-1))
    cut = own.shape[0] // 2
    first = send(across_high[:cut], along_x(-1))
    second = send(across_low[cut:], along_x(1))
    return own, low, high, across, across_high, across_low, far, first, second


def score_kernel(place, own, low, high, across, across_high, across_low, far, first, second,
                 s_own, s_hi, s_core, s_both, bias, out, keep, give):
    step = pl.program_id(0)
    mine = place[0]
    rows = out.shape[0]
    wide = own.shape[-1]
    blocks = [own, low, high, across, across_high, across_low, far]
    for k, block in enumerate(blocks):
        share = place[1 + k]
        keep[share] = block[:, mine].reshape(rows, wide)
        give[share] = block[:, 1 - mine].reshape(rows, wide)
    share = place[1 + len(blocks)]

    @pl.when(step == 0)
    def _():
        keep[share] = first[:, mine].reshape(rows, wide)
        give[share] = first[:, 1 - mine].reshape(rows, wide)

    @pl.when(step == 1)
    def _():
        keep[share] = second[:, mine].reshape(rows, wide)
        give[share] = second[:, 1 - mine].reshape(rows, wide)

    shares = keep.shape[0]
    kept = jnp.concatenate([keep[s] for s in range(shares)], axis=1)
    given = jnp.concatenate([give[s] for s in range(shares)], axis=1)
    dims = (((1,), (1,)), ((), ()))
    oris = s_own.shape[0]
    for at, (near, other) in enumerate(((s_own, s_hi), (s_core, s_both))):
        product = lax.dot_general(kept, near[...], dims, preferred_element_type=jnp.float32)
        product += lax.dot_general(given, other[...], dims, preferred_element_type=jnp.float32)
        here = slice(at * oris, (at + 1) * oris)
        out[:, here] = product + bias[:, here]


def partial_score(place, blocks, slices, bias, steps=2):
    zs, _, rows, wide = blocks[0].shape
    images = zs * rows
    take = zs // steps
    oris, width = slices[0].shape
    shares = width // wide
    whole = lambda i, place: (i, 0, 0, 0)
    fixed = lambda i, place: (0, 0, 0, 0)
    flat = lambda i, place: (0, 0)
    return pl.pallas_call(
        score_kernel,
        out_shape=(
            jax.ShapeDtypeStruct((images, 2 * oris), jnp.float32),
            jax.ShapeDtypeStruct((shares, images, wide), jnp.bfloat16),
            jax.ShapeDtypeStruct((shares, images, wide), jnp.bfloat16),
        ),
        grid_spec=pltpu.PrefetchScalarGridSpec(
            num_scalar_prefetch=1,
            grid=(steps,),
            in_specs=[pl.BlockSpec((take, 2, rows, wide), whole)] * 7
            + [pl.BlockSpec((take, 2, rows, wide), fixed)] * 2
            + [pl.BlockSpec((oris, width), flat)] * 4
            + [pl.BlockSpec((1, 2 * oris), flat)],
            out_specs=[
                pl.BlockSpec((take * rows, 2 * oris), lambda i, place: (i, 0)),
                pl.BlockSpec((shares, take * rows, wide), lambda i, place: (0, i, 0)),
                pl.BlockSpec((shares, take * rows, wide), lambda i, place: (0, i, 0)),
            ],
        ),
        compiler_params=pltpu.CompilerParams(vmem_limit_bytes=56 * MIB),
        name="score",
    )(place, *blocks, *slices, bias)


def to_row(column):
    rows = column.shape[0]
    wide = jnp.broadcast_to(column, (rows, LANES))
    square = jnp.concatenate([wide, jnp.zeros((LANES - rows, LANES), jnp.float32)], axis=0)
    return jnp.transpose(square)[0:1]


def to_column(row, rows):
    return jnp.transpose(jnp.broadcast_to(row, (LANES, LANES)))[:rows, 0:1]


def total_kernel(pieces, near, other, stats):
    total = pieces[0]
    for d in range(1, pieces.shape[0]):
        total = total + pieces[d]
    oris = near.shape[1]
    near[...] = total[:, :oris]
    other[...] = total[:, oris:]
    peak = jnp.max(total, axis=1, keepdims=True)
    mass = jnp.sum(jnp.exp(total - peak), axis=1, keepdims=True)
    both = jnp.concatenate([to_row(peak), to_row(mass), jnp.zeros((6, LANES), jnp.float32)], axis=0)
    stats[...] = jnp.broadcast_to(both[None], stats.shape)


def total_score(pieces):
    _, rows, oris = pieces.shape
    return pl.pallas_call(
        total_kernel,
        out_shape=(
            jax.ShapeDtypeStruct((rows, oris // 2), jnp.float32),
            jax.ShapeDtypeStruct((rows, oris // 2), jnp.float32),
            jax.ShapeDtypeStruct((ORI, 8, LANES), jnp.float32),
        ),
        compiler_params=pltpu.CompilerParams(vmem_limit_bytes=32 * MIB),
        name="total",
    )(pieces)


def weight_kernel(place, near, came, stats, weights, log_norm):
    rows = near.shape[0]
    core = place[0]
    used = lax.broadcasted_iota(jnp.int32, (1, LANES), 1) < rows
    peak, total = [], []
    for c in range(2):
        peaks = jnp.concatenate([stats[p, 0:1, :] for p in range(c, ORI, 2)], axis=0)
        masses = jnp.concatenate([stats[p, 1:2, :] for p in range(c, ORI, 2)], axis=0)
        top = jnp.max(peaks, axis=0, keepdims=True)
        mass = jnp.sum(masses * jnp.exp(peaks - top), axis=0, keepdims=True)
        peak.append(top)
        total.append(jnp.where(used, mass, 1.0))
        log_norm[c : c + 1, :] = top + jnp.log(total[c])
    for at, part in ((core, near), (1 - core, came)):
        top = to_column(jnp.where(at == 0, peak[0], peak[1]), rows)
        mass = to_column(jnp.where(at == 0, total[0], total[1]), rows)
        chosen = (jnp.exp(part[...] - top) / mass).astype(jnp.bfloat16)
        here = pl.ds(pl.multiple_of(at * rows, 16), rows)
        weights[:, here, :] = jnp.broadcast_to(chosen[None], (weights.shape[0], *chosen.shape))


def weigh(place, near, came, stats):
    rows, oris = near.shape
    vmem = pl.BlockSpec(memory_space=pltpu.VMEM)
    return pl.pallas_call(
        weight_kernel,
        out_shape=(
            jax.ShapeDtypeStruct((DOM, 2 * rows, oris), jnp.bfloat16),
            jax.ShapeDtypeStruct((2, LANES), jnp.float32),
        ),
        in_specs=[pl.BlockSpec(memory_space=pltpu.SMEM), vmem, vmem, vmem],
        out_specs=(vmem, vmem),
        compiler_params=pltpu.CompilerParams(vmem_limit_bytes=32 * MIB),
        name="weigh",
    )(place, near, came, stats)


def project_kernel(place, weights, keep, from_core, from_hi, from_both, out, turned):
    rows = weights.shape[1] // 2
    images = keep.shape[1]

    @pl.when(pl.program_id(0) == 0)
    def _():
        for at in range(4):
            hi = place[0] if at < 2 else 1 - place[0]
            core = place[1] if at % 2 == 0 else 1 - place[1]
            part = weights[pl.ds(hi * HALF, HALF), pl.ds(pl.multiple_of(core * rows, 16), rows), :]
            turned[:, at * images : (at + 1) * images] = jnp.transpose(part.reshape(images, part.shape[-1]))

    block = jnp.concatenate([keep[0], from_core[0], from_hi[0], from_both[0]], axis=0)
    out[...] = jnp.dot(turned[...], block, preferred_element_type=jnp.float32)


def project(place, weights, columns):
    shares, images, wide = columns[0].shape
    oris = weights.shape[-1]
    return pl.pallas_call(
        project_kernel,
        out_shape=jax.ShapeDtypeStruct((oris, shares * wide), jnp.float32),
        grid_spec=pltpu.PrefetchScalarGridSpec(
            num_scalar_prefetch=1,
            grid=(shares,),
            in_specs=[pl.BlockSpec(weights.shape, lambda i, place: (0, 0, 0))]
            + [pl.BlockSpec((1, images, wide), lambda i, place: (i, 0, 0))] * 4,
            out_specs=pl.BlockSpec((oris, wide), lambda i, place: (0, i)),
            scratch_shapes=[pltpu.VMEM((oris, 4 * images), jnp.bfloat16)],
        ),
        compiler_params=pltpu.CompilerParams(vmem_limit_bytes=56 * MIB),
        name="project",
    )(place, weights, *columns)


def squares(block):
    block = block.astype(jnp.float32)
    return jnp.sum(block * block, axis=1)


def on_device(images, shifts, slices, class_of, log_prior):
    rows = images.shape[0] // 2
    oris = slices.shape[0]
    orient = lax.axis_index("orient")
    dom = lax.axis_index("dom")
    core, x, y_lo = orient % 2, orient // 2 % RING, orient // 8
    hi, z = dom // HALF, dom % HALF

    s_hi = lax.ppermute(slices, "dom", Y_HIGH)
    s_core = lax.ppermute(slices, "orient", CORE)
    s_both = lax.ppermute(s_hi, "orient", CORE)
    onehot = class_of[:, None] == jnp.arange(log_prior.shape[0], dtype=jnp.int32)[None, :]
    prior = jnp.sum(jnp.where(onehot, log_prior[None, :], 0.0), axis=1)
    prior = jnp.concatenate([prior, lax.ppermute(prior, "orient", CORE)])
    norms = jnp.concatenate([squares(slices) + squares(s_hi), squares(s_core) + squares(s_both)])
    bias = jnp.where(z == 0, prior, 0.0) - 0.5 * norms

    own = shift_part(images, shifts.T, y_lo * RING + x, core)
    mine = lax.all_to_all(own, "dom", 0, 0, axis_index_groups=Z_GROUPS)
    blocks = gather_shares(mine)
    here, there = y_lo * RING, (1 - y_lo) * RING
    step = lambda by: (x + by) % RING
    place = jnp.stack(
        [hi, here + x, here + step(3), here + step(1), there + x, there + step(1), there + step(3), here + step(2), there + step(2)]
    ).astype(jnp.int32)
    partial, keep, give = partial_score(place, blocks, (slices, s_hi, s_core, s_both), bias[None, :])

    from_hi = lax.ppermute(give, "dom", Y_HIGH)
    from_core = lax.ppermute(keep, "orient", CORE)
    from_both = lax.ppermute(from_hi, "orient", CORE)

    pieces = lax.all_to_all(partial.reshape(HALF, rows, 2 * oris), "dom", 0, 0, axis_index_groups=Z_GROUPS)
    near, other, stats = total_score(pieces)
    came = lax.ppermute(other, "orient", CORE)
    stats = lax.all_to_all(stats, "orient", 0, 0)
    copies, log_norm = weigh(core.astype(jnp.int32)[None], near, came, stats)
    weights = lax.all_to_all(copies, "dom", 0, 0)
    place = jnp.stack([hi, core]).astype(jnp.int32)
    projected = project(place, weights, (keep, from_core, from_hi, from_both))
    return projected, log_norm[:, :rows].reshape(2 * rows)


def solution(mesh):
    placed = (P("dom", None), P("dom", None), P("orient", "dom"), P("orient"), P())
    return jax.shard_map(
        on_device,
        mesh=mesh,
        in_specs=placed,
        out_specs=(P("orient", "dom"), P("dom")),
        check_vma=False,
    )
```

```python
import functools
import math

import jax
import jax.numpy as jnp
from jax import lax
from jax.experimental import pallas as pl
from jax.experimental.pallas import tpu as pltpu
from jax.sharding import PartitionSpec as P

BOX = 256
LANES = 128
WIDE = 256
MIB = 1 << 20

ORI = 16
DOM = 16
RING = 4
HALF = DOM // 2
Z_GROUPS = [list(range(HALF)), list(range(HALF, DOM))]
CORE = [(i, i ^ 1) for i in range(ORI)]
Y_LOW = [(i, i ^ 8) for i in range(ORI)]
Y_HIGH = [(i, i ^ 8) for i in range(DOM)]


def along_x(by):
    return [(i, i // 8 * 8 + (i // 2 + by * (1 - i % 2 * 2)) % RING * 2 + i % 2) for i in range(ORI)]


AHEAD = along_x(1)
BACK = along_x(-1)


def turn_wave(turn):
    quarter = (turn + BOX // 8) >> 6
    angle = (turn - (quarter << 6)).astype(jnp.float32) * (2.0 * math.pi / BOX)
    sq = angle * angle
    sine = angle * (1.0 + sq * (-1.0 / 6 + sq * (1.0 / 120 + sq * (-1.0 / 5040 + sq * (1.0 / 362880)))))
    cosine = 1.0 + sq * (-0.5 + sq * (1.0 / 24 + sq * (-1.0 / 720 + sq * (1.0 / 40320))))
    odd = (quarter & 1) == 1
    first = jnp.where(odd, sine, cosine)
    second = jnp.where(odd, cosine, sine)
    first = jnp.where(((quarter + 1) & 2) == 2, -first, first)
    second = jnp.where((quarter & 2) == 2, -second, second)
    return first, second


def shift_kernel(place, shifts, images, out, held, sems):
    share, core, hi = place[0], place[1], place[3]
    zs, _, rows, wide = out.shape
    shares = images.shape[1] // (2 * zs * wide)
    row = pl.ds(pl.multiple_of(core * rows, 16), rows)
    copies = []
    for at in range(2 * zs):
        column = pl.ds(pl.multiple_of((at * shares + share) * wide, wide), wide)
        copies.append(pltpu.make_async_copy(images.at[row, column], held.at[at], sems.at[at]))
        copies[at].start()

    total = shifts.shape[1]
    lane = lax.broadcasted_iota(jnp.int32, (rows, LANES), 1)
    image = lax.broadcasted_iota(jnp.int32, (rows, total), 0) + core * rows
    own = image == lax.broadcasted_iota(jnp.int32, (rows, total), 1)
    by_x = jnp.sum(jnp.where(own, shifts[0:1, :], 0), axis=1, keepdims=True)
    by_y = jnp.sum(jnp.where(own, shifts[1:2, :], 0), axis=1, keepdims=True)
    freq_y = (lane // 2) * (2 * shares) + lane % 2 + 2 * share - place[2]
    cx, sx = turn_wave((lane * by_x) & (BOX - 1))
    cos_y, sin_y = turn_wave((freq_y * by_y) & (BOX - 1))
    for z in range(zs):
        copies[z].wait()
        copies[z + zs].wait()
        for part in range(2):
            pick = 2 * z + part
            cy = cos_y[:, pick : pick + 1]
            sy = sin_y[:, pick : pick + 1]
            cosine = cx * cy - sx * sy
            sine = sx * cy + cx * sy
            here = slice(part * LANES, (part + 1) * LANES)
            re = held[z, :, here].astype(jnp.float32)
            im = held[z + zs, :, here].astype(jnp.float32)
            out[z, hi, :, here] = (re * cosine + im * sine).astype(jnp.bfloat16)
            out[z, 1 - hi, :, here] = (im * cosine - re * sine).astype(jnp.bfloat16)


def shift_part(images, shifts, share, core, hi):
    rows, width = images.shape
    rows = rows // 2
    place = jnp.stack([share, core, jnp.int32(width // 2 // 256), hi]).astype(jnp.int32)
    vmem = pl.BlockSpec(memory_space=pltpu.VMEM)
    return pl.pallas_call(
        shift_kernel,
        out_shape=jax.ShapeDtypeStruct((HALF, 2, rows, WIDE), jnp.bfloat16),
        in_specs=[pl.BlockSpec(memory_space=pltpu.SMEM), vmem, pl.BlockSpec(memory_space=pl.ANY)],
        out_specs=vmem,
        scratch_shapes=[pltpu.VMEM((DOM, rows, WIDE), jnp.bfloat16), pltpu.SemaphoreType.DMA((DOM,))],
        compiler_params=pltpu.CompilerParams(vmem_limit_bytes=16 * MIB),
        name="shift",
    )(place, shifts, images)


def score_kernel(count, place, *refs):
    blocks, refs = refs[:count], refs[count:]
    slices, refs = refs[: 4 * count], refs[4 * count :]
    before, out, keep, give, sems = refs[0], *refs[-4:]
    images, oris = out.shape
    wide = blocks[0].shape[-1]
    copies = []
    for k, block in enumerate(blocks):
        for side, filed in enumerate((keep, give)):
            copies.append(pltpu.make_async_copy(block.at[:, side], filed.at[place[k]], sems.at[2 * k + side]))
    for copy in copies:
        copy.start()
    dims = (((1,), (1,)), ((), ()))
    left = jnp.concatenate([block[:, side].reshape(images, wide) for side in range(2) for block in blocks], axis=1)
    for at in range(2):
        right = jnp.concatenate([slices[(2 * at + side) * count + k][...] for side in range(2) for k in range(count)], axis=1)
        here = slice(at * oris // 2, (at + 1) * oris // 2)
        out[:, here] = lax.dot_general(left, right, dims, preferred_element_type=jnp.float32) + before[:, here]
    for copy in copies:
        copy.wait()


def add_score(place, blocks, slices, before, filed):
    count = len(blocks)
    zs, _, rows, wide = blocks[0].shape
    oris, width = slices[0].shape
    shares = width // wide
    images = zs * rows
    every = lambda shape: pl.BlockSpec(shape, lambda i, place: (0,) * len(shape))
    chunk = lambda k: pl.BlockSpec((oris, wide), lambda i, place: (0, place[k]))
    anywhere = pl.BlockSpec(memory_space=pl.ANY)
    whole = jax.ShapeDtypeStruct((shares, zs, rows, wide), jnp.bfloat16)
    inputs = [*blocks, *(part for part in slices for _ in range(count)), before, *filed]
    return pl.pallas_call(
        functools.partial(score_kernel, count),
        out_shape=(jax.ShapeDtypeStruct((images, 2 * oris), jnp.float32), whole, whole),
        grid_spec=pltpu.PrefetchScalarGridSpec(
            num_scalar_prefetch=1,
            grid=(1,),
            in_specs=[every(block.shape) for block in blocks]
            + [chunk(k) for _ in slices for k in range(count)]
            + [every(before.shape)]
            + [anywhere] * len(filed),
            out_specs=[every((images, 2 * oris)), anywhere, anywhere],
            scratch_shapes=[pltpu.SemaphoreType.DMA((2 * count,))],
        ),
        input_output_aliases={len(inputs) - 1: 1, len(inputs): 2} if filed else {},
        compiler_params=pltpu.CompilerParams(vmem_limit_bytes=24 * MIB),
        name="score",
    )(place, *inputs)


def to_row(column):
    rows = column.shape[0]
    wide = jnp.broadcast_to(column, (rows, LANES))
    square = jnp.concatenate([wide, jnp.zeros((LANES - rows, LANES), jnp.float32)], axis=0)
    return jnp.transpose(square)[0:1]


def to_column(row, rows):
    return jnp.transpose(jnp.broadcast_to(row, (LANES, LANES)))[:rows, 0:1]


def total_kernel(pieces, near, other, stats):
    total = pieces[0]
    for d in range(1, pieces.shape[0]):
        total = total + pieces[d]
    oris = near.shape[1]
    near[...] = total[:, :oris]
    other[...] = total[:, oris:]
    peak = jnp.max(total, axis=1, keepdims=True)
    mass = jnp.sum(jnp.exp(total - peak), axis=1, keepdims=True)
    both = jnp.concatenate([to_row(peak), to_row(mass), jnp.zeros((6, LANES), jnp.float32)], axis=0)
    stats[...] = jnp.broadcast_to(both[None], stats.shape)


def total_score(pieces):
    _, rows, oris = pieces.shape
    return pl.pallas_call(
        total_kernel,
        out_shape=(
            jax.ShapeDtypeStruct((rows, oris // 2), jnp.float32),
            jax.ShapeDtypeStruct((rows, oris // 2), jnp.float32),
            jax.ShapeDtypeStruct((ORI, 8, LANES), jnp.float32),
        ),
        compiler_params=pltpu.CompilerParams(vmem_limit_bytes=32 * MIB),
        name="total",
    )(pieces)


def weight_kernel(place, near, came, stats, weights, log_norm):
    rows = near.shape[0]
    core = place[0]
    used = lax.broadcasted_iota(jnp.int32, (1, LANES), 1) < rows
    peak, total = [], []
    for c in range(2):
        peaks = jnp.concatenate([stats[p, 0:1, :] for p in range(c, ORI, 2)], axis=0)
        masses = jnp.concatenate([stats[p, 1:2, :] for p in range(c, ORI, 2)], axis=0)
        top = jnp.max(peaks, axis=0, keepdims=True)
        mass = jnp.sum(masses * jnp.exp(peaks - top), axis=0, keepdims=True)
        peak.append(top)
        total.append(jnp.where(used, mass, 1.0))
        log_norm[c : c + 1, :] = top + jnp.log(total[c])
    for at, (c, part) in enumerate(((core, near), (1 - core, came))):
        top = to_column(jnp.where(c == 0, peak[0], peak[1]), rows)
        mass = to_column(jnp.where(c == 0, total[0], total[1]), rows)
        weights[at] = (jnp.exp(part[...] - top) / mass).astype(jnp.bfloat16)


def weigh(place, near, came, stats):
    rows, oris = near.shape
    vmem = pl.BlockSpec(memory_space=pltpu.VMEM)
    return pl.pallas_call(
        weight_kernel,
        out_shape=(
            jax.ShapeDtypeStruct((2, rows, oris), jnp.bfloat16),
            jax.ShapeDtypeStruct((2, LANES), jnp.float32),
        ),
        in_specs=[pl.BlockSpec(memory_space=pltpu.SMEM), vmem, vmem, vmem],
        out_specs=(vmem, vmem),
        compiler_params=pltpu.CompilerParams(vmem_limit_bytes=16 * MIB),
        name="weigh",
    )(place, near, came, stats)


def spread_kernel(near, other, out):
    zs = out.shape[0]
    out[:, 0:2] = jnp.broadcast_to(near[...][None], (zs, *near.shape))
    out[:, 2:4] = jnp.broadcast_to(other[...][None], (zs, *other.shape))


def spread(near, other):
    _, rows, oris = near.shape
    return pl.pallas_call(
        spread_kernel,
        out_shape=jax.ShapeDtypeStruct((HALF, 4, rows, oris), jnp.bfloat16),
        compiler_params=pltpu.CompilerParams(vmem_limit_bytes=16 * MIB),
        name="spread",
    )(near, other)


def project_kernel(weights, *refs):
    columns, out = refs[:-1], refs[-1]
    zs, groups, rows, oris = weights.shape
    images = zs * rows
    left = jnp.concatenate([weights[:, g].reshape(images, oris) for g in range(groups)], axis=0)
    right = []
    for column in columns:
        take, _, _, wide = column.shape
        right.append(jnp.concatenate([column[s].reshape(images, wide) for s in range(take)], axis=1))
    right = jnp.concatenate(right, axis=0)
    out[...] = lax.dot_general(left, right, (((0,), (0,)), ((), ())), preferred_element_type=jnp.float32)


def project(weights, columns, steps=4):
    shares, zs, rows, wide = columns[0].shape
    take = shares // steps
    oris = weights.shape[-1]
    return pl.pallas_call(
        project_kernel,
        out_shape=jax.ShapeDtypeStruct((oris, shares * wide), jnp.float32),
        grid=(steps,),
        in_specs=[pl.BlockSpec(weights.shape, lambda i: (0, 0, 0, 0))]
        + [pl.BlockSpec((take, zs, rows, wide), lambda i: (i, 0, 0, 0))] * 4,
        out_specs=pl.BlockSpec((oris, take * wide), lambda i: (0, i)),
        compiler_params=pltpu.CompilerParams(vmem_limit_bytes=24 * MIB),
        name="project",
    )(weights, *columns)


def squares(block):
    block = block.astype(jnp.float32)
    return jnp.sum(block * block, axis=1)


def on_device(images, shifts, slices, class_of, log_prior):
    rows = images.shape[0] // 2
    oris = slices.shape[0]
    orient = lax.axis_index("orient")
    dom = lax.axis_index("dom")
    core, x, y_lo = orient % 2, orient // 2 % RING, orient // 8
    hi, z = dom // HALF, dom % HALF

    s_hi = lax.ppermute(slices, "dom", Y_HIGH)
    s_core = lax.ppermute(slices, "orient", CORE)
    s_both = lax.ppermute(s_hi, "orient", CORE)
    onehot = class_of[:, None] == jnp.arange(log_prior.shape[0], dtype=jnp.int32)[None, :]
    prior = jnp.sum(jnp.where(onehot, log_prior[None, :], 0.0), axis=1)
    prior = jnp.concatenate([prior, lax.ppermute(prior, "orient", CORE)])
    norms = jnp.concatenate([squares(slices) + squares(s_hi), squares(s_core) + squares(s_both)])
    bias = jnp.where(z == 0, prior, 0.0) - 0.5 * norms

    share = y_lo * RING + x
    own = shift_part(images, shifts.T, share, core, hi)
    own = lax.all_to_all(own, "dom", 0, 0, axis_index_groups=Z_GROUPS)

    send = lambda block, perm: lax.ppermute(block, "orient", perm)
    behind = send(own, AHEAD)
    front = send(own, BACK)
    across = send(own, Y_LOW)
    far = send(front, BACK)
    across_front = send(front, Y_LOW)
    across_behind = send(across, AHEAD)
    across_far = send(across_front, BACK)
    ahead = 1 - 2 * core
    here, there = y_lo * RING, (1 - y_lo) * RING
    step = lambda by: (x + by * ahead) % RING
    place = lambda *shares: jnp.stack(shares).astype(jnp.int32)
    parts = (slices, s_hi, s_core, s_both)
    partial, keep, give = add_score(
        place(share, here + step(-1), here + step(1), there + x), (own, behind, front, across), parts, bias[None, :], ()
    )
    partial, keep, give = add_score(
        place(here + step(2), there + step(1), there + step(-1)), (far, across_front, across_behind), parts, partial, (keep, give)
    )
    partial, keep, give = add_score(place(there + step(2)), (across_far,), parts, partial, (keep, give))

    from_hi = lax.ppermute(give, "dom", Y_HIGH)
    from_core = lax.ppermute(keep, "orient", CORE)
    pieces = lax.all_to_all(partial.reshape(HALF, rows, 2 * oris), "dom", 0, 0, axis_index_groups=Z_GROUPS)
    near, other, stats = total_score(pieces)
    came = lax.ppermute(other, "orient", CORE)
    stats = lax.all_to_all(stats, "orient", 0, 0)
    weights, log_norm = weigh(core.astype(jnp.int32)[None], near, came, stats)
    copies = spread(weights, lax.ppermute(weights, "dom", Y_HIGH))
    from_hi, _ = lax.optimization_barrier((from_hi, copies))
    from_both = lax.ppermute(from_hi, "orient", CORE)
    weights = lax.all_to_all(copies, "dom", 0, 0, axis_index_groups=Z_GROUPS)
    projected = project(weights, (keep, from_core, from_hi, from_both))
    return projected, log_norm[:, :rows].reshape(2 * rows)


def solution(mesh):
    placed = (P("dom", None), P("dom", None), P("orient", "dom"), P("orient"), P())
    return jax.shard_map(
        on_device,
        mesh=mesh,
        in_specs=placed,
        out_specs=(P("orient", "dom"), P("dom")),
        check_vma=False,
    )
```

```python
import functools
import math

import jax
import jax.numpy as jnp
from jax import lax
from jax.experimental import pallas as pl
from jax.experimental.pallas import tpu as pltpu
from jax.sharding import PartitionSpec as P

BOX = 256
LANES = 128
WIDE = 256
MIB = 1 << 20

ORI = 16
DOM = 16
RING = 4
HALF = DOM // 2
Z_GROUPS = [list(range(HALF)), list(range(HALF, DOM))]
CORE = [(i, i ^ 1) for i in range(ORI)]
Y_LOW = [(i, i ^ 8) for i in range(ORI)]
Y_HIGH = [(i, i ^ 8) for i in range(DOM)]


def along_x(by):
    return [(i, i // 8 * 8 + (i // 2 + by * (1 - i % 2 * 2)) % RING * 2 + i % 2) for i in range(ORI)]


def along_z(by):
    pairs = []
    for o in range(ORI):
        for d in range(DOM):
            z = (d % HALF + by * (1 - o % 2 * 2)) % HALF
            pairs.append((o * DOM + d, o * DOM + d // HALF * HALF + z))
    return pairs


AHEAD = along_x(1)
BACK = along_x(-1)


def turn_wave(turn):
    quarter = (turn + BOX // 8) >> 6
    angle = (turn - (quarter << 6)).astype(jnp.float32) * (2.0 * math.pi / BOX)
    sq = angle * angle
    sine = angle * (1.0 + sq * (-1.0 / 6 + sq * (1.0 / 120 + sq * (-1.0 / 5040 + sq * (1.0 / 362880)))))
    cosine = 1.0 + sq * (-0.5 + sq * (1.0 / 24 + sq * (-1.0 / 720 + sq * (1.0 / 40320))))
    odd = (quarter & 1) == 1
    first = jnp.where(odd, sine, cosine)
    second = jnp.where(odd, cosine, sine)
    first = jnp.where(((quarter + 1) & 2) == 2, -first, first)
    second = jnp.where((quarter & 2) == 2, -second, second)
    return first, second


def shift_kernel(place, shifts, images, out, held, sems):
    share, core, hi = place[0], place[1], place[3]
    zs, _, rows, wide = out.shape
    shares = images.shape[1] // (2 * zs * wide)
    row = pl.ds(pl.multiple_of(core * rows, 16), rows)
    copies = []
    for at in range(2 * zs):
        column = pl.ds(pl.multiple_of((at * shares + share) * wide, wide), wide)
        copies.append(pltpu.make_async_copy(images.at[row, column], held.at[at], sems.at[at]))
        copies[at].start()

    total = shifts.shape[1]
    lane = lax.broadcasted_iota(jnp.int32, (rows, LANES), 1)
    image = lax.broadcasted_iota(jnp.int32, (rows, total), 0) + core * rows
    own = image == lax.broadcasted_iota(jnp.int32, (rows, total), 1)
    by_x = jnp.sum(jnp.where(own, shifts[0:1, :], 0), axis=1, keepdims=True)
    by_y = jnp.sum(jnp.where(own, shifts[1:2, :], 0), axis=1, keepdims=True)
    freq_y = (lane // 2) * (2 * shares) + lane % 2 + 2 * share - place[2]
    cx, sx = turn_wave((lane * by_x) & (BOX - 1))
    cos_y, sin_y = turn_wave((freq_y * by_y) & (BOX - 1))
    for z in range(zs):
        copies[z].wait()
        copies[z + zs].wait()
        for part in range(2):
            pick = 2 * z + part
            cy = cos_y[:, pick : pick + 1]
            sy = sin_y[:, pick : pick + 1]
            cosine = cx * cy - sx * sy
            sine = sx * cy + cx * sy
            here = slice(part * LANES, (part + 1) * LANES)
            re = held[z, :, here].astype(jnp.float32)
            im = held[z + zs, :, here].astype(jnp.float32)
            out[z, hi, :, here] = (re * cosine + im * sine).astype(jnp.bfloat16)
            out[z, 1 - hi, :, here] = (im * cosine - re * sine).astype(jnp.bfloat16)


def shift_part(images, shifts, share, core, hi):
    rows, width = images.shape
    rows = rows // 2
    place = jnp.stack([share, core, jnp.int32(width // 2 // 256), hi]).astype(jnp.int32)
    vmem = pl.BlockSpec(memory_space=pltpu.VMEM)
    return pl.pallas_call(
        shift_kernel,
        out_shape=jax.ShapeDtypeStruct((HALF, 2, rows, WIDE), jnp.bfloat16),
        in_specs=[pl.BlockSpec(memory_space=pltpu.SMEM), vmem, pl.BlockSpec(memory_space=pl.ANY)],
        out_specs=vmem,
        scratch_shapes=[pltpu.VMEM((DOM, rows, WIDE), jnp.bfloat16), pltpu.SemaphoreType.DMA((DOM,))],
        compiler_params=pltpu.CompilerParams(vmem_limit_bytes=60 * MIB),
        name="shift",
    )(place, shifts, images)


def score_kernel(count, place, *refs):
    blocks, refs = refs[:count], refs[count:]
    slices, refs = refs[: 4 * count], refs[4 * count :]
    before, out, keep, give, sems = refs[0], *refs[-4:]
    images, oris = out.shape
    wide = blocks[0].shape[-1]
    copies = []
    for k, block in enumerate(blocks):
        for side, filed in enumerate((keep, give)):
            copies.append(pltpu.make_async_copy(block.at[:, side], filed.at[place[k]], sems.at[2 * k + side]))
    for copy in copies:
        copy.start()
    dims = (((1,), (1,)), ((), ()))
    left = jnp.concatenate([block[:, side].reshape(images, wide) for side in range(2) for block in blocks], axis=1)
    for at in range(2):
        right = jnp.concatenate([slices[(2 * at + side) * count + k][...] for side in range(2) for k in range(count)], axis=1)
        here = slice(at * oris // 2, (at + 1) * oris // 2)
        out[:, here] = lax.dot_general(left, right, dims, preferred_element_type=jnp.float32) + before[:, here]
    for copy in copies:
        copy.wait()


def add_score(place, blocks, slices, before, filed):
    count = len(blocks)
    zs, _, rows, wide = blocks[0].shape
    oris, width = slices[0].shape
    shares = width // wide
    images = zs * rows
    every = lambda shape: pl.BlockSpec(shape, lambda i, place: (0,) * len(shape))
    chunk = lambda k: pl.BlockSpec((oris, wide), lambda i, place: (0, place[k]))
    anywhere = pl.BlockSpec(memory_space=pl.ANY)
    whole = pltpu.HBM((shares, zs, rows, wide), jnp.bfloat16)
    total = (pltpu.HBM if count == 1 else jax.ShapeDtypeStruct)((images, 2 * oris), jnp.float32)
    inputs = [*blocks, *(part for part in slices for _ in range(count)), before, *filed]
    return pl.pallas_call(
        functools.partial(score_kernel, count),
        out_shape=(total, whole, whole),
        grid_spec=pltpu.PrefetchScalarGridSpec(
            num_scalar_prefetch=1,
            grid=(1,),
            in_specs=[every(block.shape) for block in blocks]
            + [chunk(k) for _ in slices for k in range(count)]
            + [every(before.shape)]
            + [anywhere] * len(filed),
            out_specs=[every((images, 2 * oris)), anywhere, anywhere],
            scratch_shapes=[pltpu.SemaphoreType.DMA((2 * count,))],
        ),
        input_output_aliases={len(inputs) - 1: 1, len(inputs): 2} if filed else {},
        compiler_params=pltpu.CompilerParams(vmem_limit_bytes=24 * MIB),
        name="score",
    )(place, *inputs)


def to_row(column):
    rows = column.shape[0]
    wide = jnp.broadcast_to(column, (rows, LANES))
    square = jnp.concatenate([wide, jnp.zeros((LANES - rows, LANES), jnp.float32)], axis=0)
    return jnp.transpose(square)[0:1]


def to_column(row, rows):
    return jnp.transpose(jnp.broadcast_to(row, (LANES, LANES)))[:rows, 0:1]


def total_kernel(pieces, near, other, stats):
    total = pieces[0]
    for d in range(1, pieces.shape[0]):
        total = total + pieces[d]
    oris = near.shape[1]
    near[...] = total[:, :oris]
    other[...] = total[:, oris:]
    peak = jnp.max(total, axis=1, keepdims=True)
    mass = jnp.sum(jnp.exp(total - peak), axis=1, keepdims=True)
    both = jnp.concatenate([to_row(peak), to_row(mass), jnp.zeros((6, LANES), jnp.float32)], axis=0)
    stats[...] = jnp.broadcast_to(both[None], stats.shape)


def total_score(pieces):
    _, rows, oris = pieces.shape
    return pl.pallas_call(
        total_kernel,
        out_shape=(
            jax.ShapeDtypeStruct((rows, oris // 2), jnp.float32),
            jax.ShapeDtypeStruct((rows, oris // 2), jnp.float32),
            jax.ShapeDtypeStruct((ORI, 8, LANES), jnp.float32),
        ),
        compiler_params=pltpu.CompilerParams(vmem_limit_bytes=32 * MIB),
        name="total",
    )(pieces)


def weight_kernel(place, near, came, stats, weights, log_norm):
    rows = near.shape[0]
    core = place[0]
    used = lax.broadcasted_iota(jnp.int32, (1, LANES), 1) < rows
    peak, total = [], []
    for c in range(2):
        peaks = jnp.concatenate([stats[p, 0:1, :] for p in range(c, ORI, 2)], axis=0)
        masses = jnp.concatenate([stats[p, 1:2, :] for p in range(c, ORI, 2)], axis=0)
        top = jnp.max(peaks, axis=0, keepdims=True)
        mass = jnp.sum(masses * jnp.exp(peaks - top), axis=0, keepdims=True)
        peak.append(top)
        total.append(jnp.where(used, mass, 1.0))
        log_norm[c : c + 1, :] = top + jnp.log(total[c])
    for at, (c, part) in enumerate(((core, near), (1 - core, came))):
        top = to_column(jnp.where(c == 0, peak[0], peak[1]), rows)
        mass = to_column(jnp.where(c == 0, total[0], total[1]), rows)
        weights[at] = (jnp.exp(part[...] - top) / mass).astype(jnp.bfloat16)


def weigh(place, near, came, stats):
    rows, oris = near.shape
    vmem = pl.BlockSpec(memory_space=pltpu.VMEM)
    return pl.pallas_call(
        weight_kernel,
        out_shape=(
            jax.ShapeDtypeStruct((2, rows, oris), jnp.bfloat16),
            jax.ShapeDtypeStruct((2, LANES), jnp.float32),
        ),
        in_specs=[pl.BlockSpec(memory_space=pltpu.SMEM), vmem, vmem, vmem],
        out_specs=(vmem, vmem),
        compiler_params=pltpu.CompilerParams(vmem_limit_bytes=16 * MIB),
        name="weigh",
    )(place, near, came, stats)


def project_kernel(place, *refs):
    zs = HALF
    weights, columns, (out, left) = refs[:zs], refs[zs:-2], refs[-2:]
    groups, rows, oris = weights[0].shape
    images = zs * rows

    @pl.when(pl.program_id(0) == 0)
    def _():
        for k, block in enumerate(weights):
            z = lax.rem(place[0] + zs - k * place[1], zs)
            for g in range(groups):
                left[pl.ds(pl.multiple_of(g * images + z * rows, 16), rows), :] = block[g]

    right = []
    for column in columns:
        take, _, _, wide = column.shape
        right.append(jnp.concatenate([column[s].reshape(images, wide) for s in range(take)], axis=1))
    right = jnp.concatenate(right, axis=0)
    out[...] = lax.dot_general(left[...], right, (((0,), (0,)), ((), ())), preferred_element_type=jnp.float32)


def project(place, weights, columns, steps=4):
    shares, zs, rows, wide = columns[0].shape
    take = shares // steps
    groups, _, oris = weights[0].shape
    return pl.pallas_call(
        project_kernel,
        out_shape=jax.ShapeDtypeStruct((oris, shares * wide), jnp.float32),
        grid_spec=pltpu.PrefetchScalarGridSpec(
            num_scalar_prefetch=1,
            grid=(steps,),
            in_specs=[pl.BlockSpec((groups, rows, oris), lambda i, place: (0, 0, 0))] * zs
            + [pl.BlockSpec((take, zs, rows, wide), lambda i, place: (i, 0, 0, 0))] * 4,
            out_specs=pl.BlockSpec((oris, take * wide), lambda i, place: (0, i)),
            scratch_shapes=[pltpu.VMEM((groups * zs * rows, oris), jnp.bfloat16)],
        ),
        compiler_params=pltpu.CompilerParams(vmem_limit_bytes=60 * MIB),
        name="project",
    )(place, *weights, *columns)


def squares(block):
    block = block.astype(jnp.float32)
    return jnp.sum(block * block, axis=1)


def on_device(images, shifts, slices, class_of, log_prior):
    rows = images.shape[0] // 2
    oris = slices.shape[0]
    orient = lax.axis_index("orient")
    dom = lax.axis_index("dom")
    core, x, y_lo = orient % 2, orient // 2 % RING, orient // 8
    hi, z = dom // HALF, dom % HALF

    s_hi = lax.ppermute(slices, "dom", Y_HIGH)
    s_core = lax.ppermute(slices, "orient", CORE)
    s_both = lax.ppermute(s_hi, "orient", CORE)
    onehot = class_of[:, None] == jnp.arange(log_prior.shape[0], dtype=jnp.int32)[None, :]
    prior = jnp.sum(jnp.where(onehot, log_prior[None, :], 0.0), axis=1)
    prior = jnp.concatenate([prior, lax.ppermute(prior, "orient", CORE)])
    norms = jnp.concatenate([squares(slices) + squares(s_hi), squares(s_core) + squares(s_both)])
    bias = jnp.where(z == 0, prior, 0.0) - 0.5 * norms

    share = y_lo * RING + x
    own = shift_part(images, shifts.T, share, core, hi)
    own = lax.all_to_all(own, "dom", 0, 0, axis_index_groups=Z_GROUPS)

    send = lambda block, perm: lax.ppermute(block, "orient", perm)
    behind = send(own, AHEAD)
    front = send(own, BACK)
    across = send(own, Y_LOW)
    far = send(front, BACK)
    across_front = send(front, Y_LOW)
    across_behind = send(across, AHEAD)
    across_far = send(across_front, BACK)
    ahead = 1 - 2 * core
    here, there = y_lo * RING, (1 - y_lo) * RING
    step = lambda by: (x + by * ahead) % RING
    place = lambda *shares: jnp.stack(shares).astype(jnp.int32)
    parts = (slices, s_hi, s_core, s_both)
    partial, keep, give = add_score(
        place(share, here + step(-1), here + step(1), there + x), (own, behind, front, across), parts, bias[None, :], ()
    )
    partial, keep, give = add_score(
        place(here + step(2), there + step(1), there + step(-1)), (far, across_front, across_behind), parts, partial, (keep, give)
    )
    partial, keep, give = add_score(place(there + step(2)), (across_far,), parts, partial, (keep, give))

    from_hi = lax.ppermute(give, "dom", Y_HIGH)
    from_core = lax.ppermute(keep, "orient", CORE)
    pieces = lax.all_to_all(partial.reshape(HALF, rows, 2 * oris), "dom", 0, 0, axis_index_groups=Z_GROUPS)
    near, other, stats = total_score(pieces)
    came = lax.ppermute(other, "orient", CORE)
    stats = lax.all_to_all(stats, "orient", 0, 0)
    weights, log_norm = weigh(core.astype(jnp.int32)[None], near, came, stats)
    weights = jnp.concatenate([weights, lax.ppermute(weights, "dom", Y_HIGH)])
    from_hi, _ = lax.optimization_barrier((from_hi, weights))
    from_both = lax.ppermute(from_hi, "orient", CORE)

    around = lambda by, block: lax.ppermute(block, ("orient", "dom"), along_z(by))
    one, back_one = around(1, weights), around(-1, weights)
    two, back_two = around(2, weights), around(-2, weights)
    three, back_three = around(2, one), around(-2, back_one)
    four = around(2, two)
    weights = (weights, one, two, three, four, back_three, back_two, back_one)
    projected = project(place(z, ahead), weights, (keep, from_core, from_hi, from_both))
    return projected, log_norm[:, :rows].reshape(2 * rows)


def solution(mesh):
    placed = (P("dom", None), P("dom", None), P("orient", "dom"), P("orient"), P())
    return jax.shard_map(
        on_device,
        mesh=mesh,
        in_specs=placed,
        out_specs=(P("orient", "dom"), P("dom")),
        check_vma=False,
    )
```

```python
import functools
import math

import jax
import jax.numpy as jnp
from jax import lax
from jax.experimental import pallas as pl
from jax.experimental.pallas import tpu as pltpu
from jax.sharding import PartitionSpec as P

BOX = 256
LANES = 128
WIDE = 256
MIB = 1 << 20

ORI = 16
DOM = 16
RING = 4
HALF = DOM // 2
Z_GROUPS = [list(range(HALF)), list(range(HALF, DOM))]
CORE = [(i, i ^ 1) for i in range(ORI)]
Y_LOW = [(i, i ^ 8) for i in range(ORI)]
Y_HIGH = [(i, i ^ 8) for i in range(DOM)]
CORE_HIGH = [(i, i ^ (DOM + 8)) for i in range(ORI * DOM)]


def along_x(by):
    return [(i, i // 8 * 8 + (i // 2 + by * (1 - i % 2 * 2)) % RING * 2 + i % 2) for i in range(ORI)]


def along_z(by):
    pairs = []
    for o in range(ORI):
        for d in range(DOM):
            z = (d % HALF + by * (1 - o % 2 * 2)) % HALF
            pairs.append((o * DOM + d, o * DOM + d // HALF * HALF + z))
    return pairs


AHEAD = along_x(1)
BACK = along_x(-1)


def turn_wave(turn):
    quarter = (turn + BOX // 8) >> 6
    angle = (turn - (quarter << 6)).astype(jnp.float32) * (2.0 * math.pi / BOX)
    sq = angle * angle
    sine = angle * (1.0 + sq * (-1.0 / 6 + sq * (1.0 / 120 + sq * (-1.0 / 5040 + sq * (1.0 / 362880)))))
    cosine = 1.0 + sq * (-0.5 + sq * (1.0 / 24 + sq * (-1.0 / 720 + sq * (1.0 / 40320))))
    odd = (quarter & 1) == 1
    first = jnp.where(odd, sine, cosine)
    second = jnp.where(odd, cosine, sine)
    first = jnp.where(((quarter + 1) & 2) == 2, -first, first)
    second = jnp.where((quarter & 2) == 2, -second, second)
    return first, second


def shift_kernel(place, shifts, images, out, held, sems):
    share, core, hi = place[0], place[1], place[3]
    zs, _, rows, wide = out.shape
    shares = images.shape[1] // (2 * zs * wide)
    row = pl.ds(pl.multiple_of(core * rows, 16), rows)
    copies = []
    for at in range(2 * zs):
        column = pl.ds(pl.multiple_of((at * shares + share) * wide, wide), wide)
        copies.append(pltpu.make_async_copy(images.at[row, column], held.at[at], sems.at[at]))
        copies[at].start()

    total = shifts.shape[1]
    lane = lax.broadcasted_iota(jnp.int32, (rows, LANES), 1)
    image = lax.broadcasted_iota(jnp.int32, (rows, total), 0) + core * rows
    own = image == lax.broadcasted_iota(jnp.int32, (rows, total), 1)
    by_x = jnp.sum(jnp.where(own, shifts[0:1, :], 0), axis=1, keepdims=True)
    by_y = jnp.sum(jnp.where(own, shifts[1:2, :], 0), axis=1, keepdims=True)
    freq_y = (lane // 2) * (2 * shares) + lane % 2 + 2 * share - place[2]
    cx, sx = turn_wave((lane * by_x) & (BOX - 1))
    cos_y, sin_y = turn_wave((freq_y * by_y) & (BOX - 1))
    for z in range(zs):
        copies[z].wait()
        copies[z + zs].wait()
        for part in range(2):
            pick = 2 * z + part
            cy = cos_y[:, pick : pick + 1]
            sy = sin_y[:, pick : pick + 1]
            cosine = cx * cy - sx * sy
            sine = sx * cy + cx * sy
            here = slice(part * LANES, (part + 1) * LANES)
            re = held[z, :, here].astype(jnp.float32)
            im = held[z + zs, :, here].astype(jnp.float32)
            out[z, hi, :, here] = (re * cosine + im * sine).astype(jnp.bfloat16)
            out[z, 1 - hi, :, here] = (im * cosine - re * sine).astype(jnp.bfloat16)


def shift_part(images, shifts, share, core, hi):
    rows, width = images.shape
    rows = rows // 2
    place = jnp.stack([share, core, jnp.int32(width // 2 // 256), hi]).astype(jnp.int32)
    vmem = pl.BlockSpec(memory_space=pltpu.VMEM)
    return pl.pallas_call(
        shift_kernel,
        out_shape=jax.ShapeDtypeStruct((HALF, 2, rows, WIDE), jnp.bfloat16),
        in_specs=[pl.BlockSpec(memory_space=pltpu.SMEM), vmem, pl.BlockSpec(memory_space=pl.ANY)],
        out_specs=vmem,
        scratch_shapes=[pltpu.VMEM((DOM, rows, WIDE), jnp.bfloat16), pltpu.SemaphoreType.DMA((DOM,))],
        compiler_params=pltpu.CompilerParams(vmem_limit_bytes=60 * MIB),
        name="shift",
    )(place, shifts, images)


def score_kernel(count, place, *refs):
    blocks, refs = refs[:count], refs[count:]
    slices, refs = refs[: 4 * count], refs[4 * count :]
    before, out, keep, give, sems = refs[0], *refs[-4:]
    images, oris = out.shape
    wide = blocks[0].shape[-1]
    copies = []
    for k, block in enumerate(blocks):
        for side, filed in enumerate((keep, give)):
            copies.append(pltpu.make_async_copy(block.at[:, side], filed.at[place[k]], sems.at[2 * k + side]))
    for copy in copies:
        copy.start()
    dims = (((1,), (1,)), ((), ()))
    left = jnp.concatenate([block[:, side].reshape(images, wide) for side in range(2) for block in blocks], axis=1)
    for at in range(2):
        right = jnp.concatenate([slices[(2 * at + side) * count + k][...] for side in range(2) for k in range(count)], axis=1)
        here = slice(at * oris // 2, (at + 1) * oris // 2)
        out[:, here] = lax.dot_general(left, right, dims, preferred_element_type=jnp.float32) + before[:, here]
    for copy in copies:
        copy.wait()


def add_score(place, blocks, slices, before, filed):
    count = len(blocks)
    zs, _, rows, wide = blocks[0].shape
    oris, width = slices[0].shape
    shares = width // wide
    images = zs * rows
    every = lambda shape: pl.BlockSpec(shape, lambda i, place: (0,) * len(shape))
    chunk = lambda k: pl.BlockSpec((oris, wide), lambda i, place: (0, place[k]))
    anywhere = pl.BlockSpec(memory_space=pl.ANY)
    whole = pltpu.HBM((shares, zs, rows, wide), jnp.bfloat16)
    total = (pltpu.HBM if count == 1 else jax.ShapeDtypeStruct)((images, 2 * oris), jnp.float32)
    inputs = [*blocks, *(part for part in slices for _ in range(count)), before, *filed]
    return pl.pallas_call(
        functools.partial(score_kernel, count),
        out_shape=(total, whole, whole),
        grid_spec=pltpu.PrefetchScalarGridSpec(
            num_scalar_prefetch=1,
            grid=(1,),
            in_specs=[every(block.shape) for block in blocks]
            + [chunk(k) for _ in slices for k in range(count)]
            + [every(before.shape)]
            + [anywhere] * len(filed),
            out_specs=[every((images, 2 * oris)), anywhere, anywhere],
            scratch_shapes=[pltpu.SemaphoreType.DMA((2 * count,))],
        ),
        input_output_aliases={len(inputs) - 1: 1, len(inputs): 2} if filed else {},
        compiler_params=pltpu.CompilerParams(vmem_limit_bytes=24 * MIB),
        name="score",
    )(place, *inputs)


def to_row(column):
    rows = column.shape[0]
    wide = jnp.broadcast_to(column, (rows, LANES))
    square = jnp.concatenate([wide, jnp.zeros((LANES - rows, LANES), jnp.float32)], axis=0)
    return jnp.transpose(square)[0:1]


def to_column(row, rows):
    return jnp.transpose(jnp.broadcast_to(row, (LANES, LANES)))[:rows, 0:1]


def total_kernel(pieces, near, other, stats):
    total = pieces[0]
    for d in range(1, pieces.shape[0]):
        total = total + pieces[d]
    oris = near.shape[1]
    near[...] = total[:, :oris]
    other[...] = total[:, oris:]
    peak = jnp.max(total, axis=1, keepdims=True)
    mass = jnp.sum(jnp.exp(total - peak), axis=1, keepdims=True)
    both = jnp.concatenate([to_row(peak), to_row(mass), jnp.zeros((6, LANES), jnp.float32)], axis=0)
    stats[...] = jnp.broadcast_to(both[None], stats.shape)


def total_score(pieces):
    _, rows, oris = pieces.shape
    return pl.pallas_call(
        total_kernel,
        out_shape=(
            jax.ShapeDtypeStruct((rows, oris // 2), jnp.float32),
            jax.ShapeDtypeStruct((rows, oris // 2), jnp.float32),
            jax.ShapeDtypeStruct((ORI, 8, LANES), jnp.float32),
        ),
        compiler_params=pltpu.CompilerParams(vmem_limit_bytes=32 * MIB),
        name="total",
    )(pieces)


def weight_kernel(place, near, came, near_hi, came_hi, stats, stats_hi, weights, log_norm):
    rows = near.shape[0]
    core = place[0]
    used = lax.broadcasted_iota(jnp.int32, (1, LANES), 1) < rows
    peak, total = [], []
    for hi, given in enumerate((stats, stats_hi)):
        for c in range(2):
            peaks = jnp.concatenate([given[p, 0:1, :] for p in range(c, ORI, 2)], axis=0)
            masses = jnp.concatenate([given[p, 1:2, :] for p in range(c, ORI, 2)], axis=0)
            top = jnp.max(peaks, axis=0, keepdims=True)
            mass = jnp.sum(masses * jnp.exp(peaks - top), axis=0, keepdims=True)
            peak.append(top)
            total.append(jnp.where(used, mass, 1.0))
            if hi == 0:
                log_norm[c : c + 1, :] = top + jnp.log(total[c])
    for at, part in enumerate((near, came, near_hi, came_hi)):
        first = (core if at % 2 == 0 else 1 - core) == 0
        hi = 2 * (at // 2)
        top = to_column(jnp.where(first, peak[hi], peak[hi + 1]), rows)
        mass = to_column(jnp.where(first, total[hi], total[hi + 1]), rows)
        weights[at] = (jnp.exp(part[...] - top) / mass).astype(jnp.bfloat16)


def weigh(place, scores, stats, stats_hi):
    rows, oris = scores[0].shape
    vmem = pl.BlockSpec(memory_space=pltpu.VMEM)
    return pl.pallas_call(
        weight_kernel,
        out_shape=(
            jax.ShapeDtypeStruct((4, rows, oris), jnp.bfloat16),
            jax.ShapeDtypeStruct((2, LANES), jnp.float32),
        ),
        in_specs=[pl.BlockSpec(memory_space=pltpu.SMEM)] + [vmem] * 6,
        out_specs=(vmem, vmem),
        compiler_params=pltpu.CompilerParams(vmem_limit_bytes=16 * MIB),
        name="weigh",
    )(place, *scores, stats, stats_hi)


def stage_kernel(*refs):
    columns, out, sems = refs[:-2], refs[-2], refs[-1]
    copies = [pltpu.make_async_copy(column, out.at[g], sems.at[g]) for g, column in enumerate(columns)]
    for copy in copies:
        copy.start()
    for copy in copies:
        copy.wait()


def stage(*columns):
    anywhere = pl.BlockSpec(memory_space=pl.ANY)
    return pl.pallas_call(
        stage_kernel,
        out_shape=pltpu.VMEM((len(columns), *columns[0].shape), jnp.bfloat16),
        in_specs=[anywhere] * len(columns),
        out_specs=anywhere,
        scratch_shapes=[pltpu.SemaphoreType.DMA((len(columns),))],
        compiler_params=pltpu.CompilerParams(vmem_limit_bytes=16 * MIB),
        cost_estimate=pl.CostEstimate(flops=0, transcendentals=0, bytes_accessed=12 * MIB),
        name="stage",
    )(*columns)


def project_kernel(place, *refs):
    zs = HALF
    weights, columns, (out, left, done, sems) = refs[:zs], refs[zs], refs[zs + 1 :]
    groups, rows, oris = weights[0].shape
    images = zs * rows
    _, shares, _, _, wide = columns.shape
    for k, block in enumerate(weights):
        z = lax.rem(place[0] + zs - k * place[1], zs)
        for g in range(groups):
            left[pl.ds(pl.multiple_of(g * images + z * rows, 16), rows), :] = block[g]
    copies = []
    for at in range(0, shares, 2):
        right = jnp.concatenate(
            [columns[:, s].reshape(groups * images, wide) for s in (at, at + 1)], axis=1
        )
        done[at // 2] = lax.dot_general(left[...], right, (((0,), (0,)), ((), ())), preferred_element_type=jnp.float32)
        here = pl.ds(at * wide, 2 * wide)
        copies.append(pltpu.make_async_copy(done.at[at // 2], out.at[:, here], sems.at[at // 2]))
        copies[-1].start()
    for copy in copies:
        copy.wait()


def project(place, weights, columns):
    _, shares, zs, rows, wide = columns.shape
    groups, _, oris = weights[0].shape
    vmem = pl.BlockSpec(memory_space=pltpu.VMEM)
    return pl.pallas_call(
        project_kernel,
        out_shape=jax.ShapeDtypeStruct((oris, shares * wide), jnp.float32),
        in_specs=[pl.BlockSpec(memory_space=pltpu.SMEM)] + [vmem] * (len(weights) + 1),
        out_specs=pl.BlockSpec(memory_space=pl.ANY),
        scratch_shapes=[
            pltpu.VMEM((groups * zs * rows, oris), jnp.bfloat16),
            pltpu.VMEM((shares // 2, oris, 2 * wide), jnp.float32),
            pltpu.SemaphoreType.DMA((shares // 2,)),
        ],
        compiler_params=pltpu.CompilerParams(vmem_limit_bytes=32 * MIB),
        name="project",
    )(place, *weights, columns)


def squares(block):
    block = block.astype(jnp.float32)
    return jnp.sum(block * block, axis=1)


def on_device(images, shifts, slices, class_of, log_prior):
    rows = images.shape[0] // 2
    oris = slices.shape[0]
    orient = lax.axis_index("orient")
    dom = lax.axis_index("dom")
    core, x, y_lo = orient % 2, orient // 2 % RING, orient // 8
    hi, z = dom // HALF, dom % HALF

    s_hi = lax.ppermute(slices, "dom", Y_HIGH)
    s_core = lax.ppermute(slices, "orient", CORE)
    s_both = lax.ppermute(s_hi, "orient", CORE)
    onehot = class_of[:, None] == jnp.arange(log_prior.shape[0], dtype=jnp.int32)[None, :]
    prior = jnp.sum(jnp.where(onehot, log_prior[None, :], 0.0), axis=1)
    prior = jnp.concatenate([prior, lax.ppermute(prior, "orient", CORE)])
    norms = jnp.concatenate([squares(slices) + squares(s_hi), squares(s_core) + squares(s_both)])
    bias = jnp.where(z == 0, prior, 0.0) - 0.5 * norms

    share = y_lo * RING + x
    own = shift_part(images, shifts.T, share, core, hi)
    own = lax.all_to_all(own, "dom", 0, 0, axis_index_groups=Z_GROUPS)

    send = lambda block, perm: lax.ppermute(block, "orient", perm)
    behind = send(own, AHEAD)
    front = send(own, BACK)
    across = send(own, Y_LOW)
    after, _ = lax.optimization_barrier((front, behind))
    far = send(after, BACK)
    across_front = send(front, Y_LOW)
    across_behind = send(across, AHEAD)
    across_far = send(across_front, BACK)
    ahead = 1 - 2 * core
    here, there = y_lo * RING, (1 - y_lo) * RING
    step = lambda by: (x + by * ahead) % RING
    place = lambda *shares: jnp.stack(shares).astype(jnp.int32)
    parts = (slices, s_hi, s_core, s_both)
    partial, keep, give = add_score(
        place(share, here + step(-1), here + step(1), there + x), (own, behind, front, across), parts, bias[None, :], ()
    )
    partial, keep, give = add_score(
        place(here + step(2), there + step(1), there + step(-1)), (far, across_front, across_behind), parts, partial, (keep, give)
    )
    partial, keep, give = add_score(place(there + step(2)), (across_far,), parts, partial, (keep, give))

    from_hi = lax.ppermute(give, "dom", Y_HIGH)
    from_core = lax.ppermute(keep, "orient", CORE)
    pieces = lax.all_to_all(partial.reshape(HALF, rows, 2 * oris), "dom", 0, 0, axis_index_groups=Z_GROUPS)
    near, other, stats = total_score(pieces)
    both_axes = ("orient", "dom")
    stats = lax.all_to_all(stats, "orient", 0, 0)
    scores = (
        near,
        lax.ppermute(other, "orient", CORE),
        lax.ppermute(near, "dom", Y_HIGH),
        lax.ppermute(other, both_axes, CORE_HIGH),
    )
    stats, *scores = lax.optimization_barrier((stats, *scores))
    weights, log_norm = weigh(core.astype(jnp.int32)[None], scores, stats, lax.ppermute(stats, "dom", Y_HIGH))
    from_hi, _ = lax.optimization_barrier((from_hi, weights))
    from_both = lax.ppermute(from_hi, "orient", CORE)

    around = lambda by, block: lax.ppermute(block, both_axes, along_z(by))
    one, back_one = around(1, weights), around(-1, weights)
    two, back_two = around(2, weights), around(-2, weights)
    three, back_three = around(2, one), around(-2, back_one)
    four = around(2, two)
    weights = (weights, one, two, three, four, back_three, back_two, back_one)
    projected = project(place(z, ahead), weights, stage(keep, from_core, from_hi, from_both))
    return projected, log_norm[:, :rows].reshape(2 * rows)


def solution(mesh):
    placed = (P("dom", None), P("dom", None), P("orient", "dom"), P("orient"), P())
    return jax.shard_map(
        on_device,
        mesh=mesh,
        in_specs=placed,
        out_specs=(P("orient", "dom"), P("dom")),
        check_vma=False,
    )
```

```python
import functools
import math

import jax
import jax.numpy as jnp
from jax import lax
from jax.experimental import pallas as pl
from jax.experimental.pallas import tpu as pltpu
from jax.sharding import PartitionSpec as P

BOX = 256
LANES = 128
WIDE = 256
MIB = 1 << 20

ORI = 16
DOM = 16
RING = 4
HALF = DOM // 2
Z_GROUPS = [list(range(HALF)), list(range(HALF, DOM))]
CORE = [(i, i ^ 1) for i in range(ORI)]
Y_LOW = [(i, i ^ 8) for i in range(ORI)]
Y_HIGH = [(i, i ^ 8) for i in range(DOM)]


def along_x(by):
    return [(i, i // 8 * 8 + (i // 2 + by * (1 - i % 2 * 2)) % RING * 2 + i % 2) for i in range(ORI)]


def along_z(by):
    pairs = []
    for o in range(ORI):
        for d in range(DOM):
            z = (d % HALF + by * (1 - o % 2 * 2)) % HALF
            pairs.append((o * DOM + d, o * DOM + d // HALF * HALF + z))
    return pairs


AHEAD = along_x(1)
BACK = along_x(-1)


def turn_wave(turn):
    quarter = (turn + BOX // 8) >> 6
    angle = (turn - (quarter << 6)).astype(jnp.float32) * (2.0 * math.pi / BOX)
    sq = angle * angle
    sine = angle * (1.0 + sq * (-1.0 / 6 + sq * (1.0 / 120 + sq * (-1.0 / 5040 + sq * (1.0 / 362880)))))
    cosine = 1.0 + sq * (-0.5 + sq * (1.0 / 24 + sq * (-1.0 / 720 + sq * (1.0 / 40320))))
    odd = (quarter & 1) == 1
    first = jnp.where(odd, sine, cosine)
    second = jnp.where(odd, cosine, sine)
    first = jnp.where(((quarter + 1) & 2) == 2, -first, first)
    second = jnp.where((quarter & 2) == 2, -second, second)
    return first, second


def shift_kernel(place, shifts, images, out, held, sems):
    share, core, hi = place[0], place[1], place[3]
    zs, _, rows, wide = out.shape
    shares = images.shape[1] // (2 * zs * wide)
    row = pl.ds(pl.multiple_of(core * rows, 16), rows)
    copies = []
    for at in range(2 * zs):
        column = pl.ds(pl.multiple_of((at * shares + share) * wide, wide), wide)
        copies.append(pltpu.make_async_copy(images.at[row, column], held.at[at], sems.at[at]))
        copies[at].start()

    total = shifts.shape[1]
    lane = lax.broadcasted_iota(jnp.int32, (rows, LANES), 1)
    image = lax.broadcasted_iota(jnp.int32, (rows, total), 0) + core * rows
    own = image == lax.broadcasted_iota(jnp.int32, (rows, total), 1)
    by_x = jnp.sum(jnp.where(own, shifts[0:1, :], 0), axis=1, keepdims=True)
    by_y = jnp.sum(jnp.where(own, shifts[1:2, :], 0), axis=1, keepdims=True)
    freq_y = (lane // 2) * (2 * shares) + lane % 2 + 2 * share - place[2]
    cx, sx = turn_wave((lane * by_x) & (BOX - 1))
    cos_y, sin_y = turn_wave((freq_y * by_y) & (BOX - 1))
    for z in range(zs):
        copies[z].wait()
        copies[z + zs].wait()
        for part in range(2):
            pick = 2 * z + part
            cy = cos_y[:, pick : pick + 1]
            sy = sin_y[:, pick : pick + 1]
            cosine = cx * cy - sx * sy
            sine = sx * cy + cx * sy
            here = slice(part * LANES, (part + 1) * LANES)
            re = held[z, :, here].astype(jnp.float32)
            im = held[z + zs, :, here].astype(jnp.float32)
            out[z, hi, :, here] = (re * cosine + im * sine).astype(jnp.bfloat16)
            out[z, 1 - hi, :, here] = (im * cosine - re * sine).astype(jnp.bfloat16)


def shift_part(images, shifts, share, core, hi):
    rows, width = images.shape
    rows = rows // 2
    place = jnp.stack([share, core, jnp.int32(width // 2 // 256), hi]).astype(jnp.int32)
    vmem = pl.BlockSpec(memory_space=pltpu.VMEM)
    return pl.pallas_call(
        shift_kernel,
        out_shape=jax.ShapeDtypeStruct((HALF, 2, rows, WIDE), jnp.bfloat16),
        in_specs=[pl.BlockSpec(memory_space=pltpu.SMEM), vmem, pl.BlockSpec(memory_space=pl.ANY)],
        out_specs=vmem,
        scratch_shapes=[pltpu.VMEM((DOM, rows, WIDE), jnp.bfloat16), pltpu.SemaphoreType.DMA((DOM,))],
        compiler_params=pltpu.CompilerParams(vmem_limit_bytes=60 * MIB),
        name="shift",
    )(place, shifts, images)


def score_kernel(count, place, *refs):
    blocks, refs = refs[:count], refs[count:]
    slices, refs = refs[: 4 * count], refs[4 * count :]
    before, out, keep, give, sems = refs[0], *refs[-4:]
    images, oris = out.shape
    wide = blocks[0].shape[-1]
    copies = []
    for k, block in enumerate(blocks):
        for side, filed in enumerate((keep, give)):
            copies.append(pltpu.make_async_copy(block.at[:, side], filed.at[place[k]], sems.at[2 * k + side]))
    for copy in copies:
        copy.start()
    dims = (((1,), (1,)), ((), ()))
    left = jnp.concatenate([block[:, side].reshape(images, wide) for side in range(2) for block in blocks], axis=1)
    for at in range(2):
        right = jnp.concatenate([slices[(2 * at + side) * count + k][...] for side in range(2) for k in range(count)], axis=1)
        here = slice(at * oris // 2, (at + 1) * oris // 2)
        out[:, here] = lax.dot_general(left, right, dims, preferred_element_type=jnp.float32) + before[:, here]
    for copy in copies:
        copy.wait()


def add_score(place, blocks, slices, before, filed):
    count = len(blocks)
    zs, _, rows, wide = blocks[0].shape
    oris, width = slices[0].shape
    shares = width // wide
    images = zs * rows
    every = lambda shape: pl.BlockSpec(shape, lambda i, place: (0,) * len(shape))
    chunk = lambda k: pl.BlockSpec((oris, wide), lambda i, place: (0, place[k]))
    anywhere = pl.BlockSpec(memory_space=pl.ANY)
    whole = pltpu.HBM((shares, zs, rows, wide), jnp.bfloat16)
    total = (pltpu.HBM if count == 1 else jax.ShapeDtypeStruct)((images, 2 * oris), jnp.float32)
    inputs = [*blocks, *(part for part in slices for _ in range(count)), before, *filed]
    return pl.pallas_call(
        functools.partial(score_kernel, count),
        out_shape=(total, whole, whole),
        grid_spec=pltpu.PrefetchScalarGridSpec(
            num_scalar_prefetch=1,
            grid=(1,),
            in_specs=[every(block.shape) for block in blocks]
            + [chunk(k) for _ in slices for k in range(count)]
            + [every(before.shape)]
            + [anywhere] * len(filed),
            out_specs=[every((images, 2 * oris)), anywhere, anywhere],
            scratch_shapes=[pltpu.SemaphoreType.DMA((2 * count,))],
        ),
        input_output_aliases={len(inputs) - 1: 1, len(inputs): 2} if filed else {},
        compiler_params=pltpu.CompilerParams(vmem_limit_bytes=24 * MIB),
        name="score",
    )(place, *inputs)


def to_row(column):
    rows = column.shape[0]
    wide = jnp.broadcast_to(column, (rows, LANES))
    square = jnp.concatenate([wide, jnp.zeros((LANES - rows, LANES), jnp.float32)], axis=0)
    return jnp.transpose(square)[0:1]


def to_column(row, rows):
    return jnp.transpose(jnp.broadcast_to(row, (LANES, LANES)))[:rows, 0:1]


def total_kernel(pieces, near, other, stats):
    total = pieces[0]
    for d in range(1, pieces.shape[0]):
        total = total + pieces[d]
    oris = near.shape[1]
    near[...] = total[:, :oris]
    other[...] = total[:, oris:]
    peak = jnp.max(total, axis=1, keepdims=True)
    mass = jnp.sum(jnp.exp(total - peak), axis=1, keepdims=True)
    both = jnp.concatenate([to_row(peak), to_row(mass), jnp.zeros((6, LANES), jnp.float32)], axis=0)
    stats[...] = jnp.broadcast_to(both[None], stats.shape)


def total_score(pieces):
    _, rows, oris = pieces.shape
    return pl.pallas_call(
        total_kernel,
        out_shape=(
            jax.ShapeDtypeStruct((rows, oris // 2), jnp.float32),
            jax.ShapeDtypeStruct((rows, oris // 2), jnp.float32),
            jax.ShapeDtypeStruct((ORI, 8, LANES), jnp.float32),
        ),
        compiler_params=pltpu.CompilerParams(vmem_limit_bytes=32 * MIB),
        name="total",
    )(pieces)


def weight_kernel(place, near, came, stats, weights, log_norm):
    rows = near.shape[0]
    core = place[0]
    used = lax.broadcasted_iota(jnp.int32, (1, LANES), 1) < rows
    peak, total = [], []
    for c in range(2):
        peaks = jnp.concatenate([stats[p, 0:1, :] for p in range(c, ORI, 2)], axis=0)
        masses = jnp.concatenate([stats[p, 1:2, :] for p in range(c, ORI, 2)], axis=0)
        top = jnp.max(peaks, axis=0, keepdims=True)
        mass = jnp.sum(masses * jnp.exp(peaks - top), axis=0, keepdims=True)
        peak.append(top)
        total.append(jnp.where(used, mass, 1.0))
        log_norm[c : c + 1, :] = top + jnp.log(total[c])
    for at, (c, part) in enumerate(((core, near), (1 - core, came))):
        top = to_column(jnp.where(c == 0, peak[0], peak[1]), rows)
        mass = to_column(jnp.where(c == 0, total[0], total[1]), rows)
        weights[at] = (jnp.exp(part[...] - top) / mass).astype(jnp.bfloat16)


def weigh(place, near, came, stats):
    rows, oris = near.shape
    vmem = pl.BlockSpec(memory_space=pltpu.VMEM)
    return pl.pallas_call(
        weight_kernel,
        out_shape=(
            jax.ShapeDtypeStruct((2, rows, oris), jnp.bfloat16),
            jax.ShapeDtypeStruct((2, LANES), jnp.float32),
        ),
        in_specs=[pl.BlockSpec(memory_space=pltpu.SMEM), vmem, vmem, vmem],
        out_specs=(vmem, vmem),
        compiler_params=pltpu.CompilerParams(vmem_limit_bytes=16 * MIB),
        name="weigh",
    )(place, near, came, stats)


def stage_kernel(*refs):
    columns, out, sems = refs[:-2], refs[-2], refs[-1]
    copies = [pltpu.make_async_copy(column, out.at[g], sems.at[g]) for g, column in enumerate(columns)]
    for copy in copies:
        copy.start()
    for copy in copies:
        copy.wait()


def stage(*columns):
    anywhere = pl.BlockSpec(memory_space=pl.ANY)
    return pl.pallas_call(
        stage_kernel,
        out_shape=pltpu.VMEM((len(columns), *columns[0].shape), jnp.bfloat16),
        in_specs=[anywhere] * len(columns),
        out_specs=anywhere,
        scratch_shapes=[pltpu.SemaphoreType.DMA((len(columns),))],
        compiler_params=pltpu.CompilerParams(vmem_limit_bytes=16 * MIB),
        cost_estimate=pl.CostEstimate(flops=0, transcendentals=0, bytes_accessed=12 * MIB),
        name="stage",
    )(*columns)


def project_kernel(place, *refs):
    zs = HALF
    weights, columns, (out, left, done, sems) = refs[:zs], refs[zs], refs[zs + 1 :]
    groups, rows, oris = weights[0].shape
    images = zs * rows
    _, shares, _, _, wide = columns.shape
    for k, block in enumerate(weights):
        z = lax.rem(place[0] + zs - k * place[1], zs)
        for g in range(groups):
            left[pl.ds(pl.multiple_of(g * images + z * rows, 16), rows), :] = block[g]
    copies = []
    for at in range(0, shares, 2):
        right = jnp.concatenate(
            [columns[:, s].reshape(groups * images, wide) for s in (at, at + 1)], axis=1
        )
        done[at // 2] = lax.dot_general(left[...], right, (((0,), (0,)), ((), ())), preferred_element_type=jnp.float32)
        here = pl.ds(at * wide, 2 * wide)
        copies.append(pltpu.make_async_copy(done.at[at // 2], out.at[:, here], sems.at[at // 2]))
        copies[-1].start()
    for copy in copies:
        copy.wait()


def project(place, weights, columns):
    _, shares, zs, rows, wide = columns.shape
    groups, _, oris = weights[0].shape
    vmem = pl.BlockSpec(memory_space=pltpu.VMEM)
    return pl.pallas_call(
        project_kernel,
        out_shape=jax.ShapeDtypeStruct((oris, shares * wide), jnp.float32),
        in_specs=[pl.BlockSpec(memory_space=pltpu.SMEM)] + [vmem] * (len(weights) + 1),
        out_specs=pl.BlockSpec(memory_space=pl.ANY),
        scratch_shapes=[
            pltpu.VMEM((groups * zs * rows, oris), jnp.bfloat16),
            pltpu.VMEM((shares // 2, oris, 2 * wide), jnp.float32),
            pltpu.SemaphoreType.DMA((shares // 2,)),
        ],
        compiler_params=pltpu.CompilerParams(vmem_limit_bytes=32 * MIB),
        name="project",
    )(place, *weights, columns)


def squares(block):
    block = block.astype(jnp.float32)
    return jnp.sum(block * block, axis=1)


def on_device(images, shifts, slices, class_of, log_prior):
    rows = images.shape[0] // 2
    oris = slices.shape[0]
    orient = lax.axis_index("orient")
    dom = lax.axis_index("dom")
    core, x, y_lo = orient % 2, orient // 2 % RING, orient // 8
    hi, z = dom // HALF, dom % HALF

    s_hi = lax.ppermute(slices, "dom", Y_HIGH)
    s_core = lax.ppermute(slices, "orient", CORE)
    s_both = lax.ppermute(s_hi, "orient", CORE)
    onehot = class_of[:, None] == jnp.arange(log_prior.shape[0], dtype=jnp.int32)[None, :]
    prior = jnp.sum(jnp.where(onehot, log_prior[None, :], 0.0), axis=1)
    prior = jnp.concatenate([prior, lax.ppermute(prior, "orient", CORE)])
    norms = jnp.concatenate([squares(slices) + squares(s_hi), squares(s_core) + squares(s_both)])
    bias = jnp.where(z == 0, prior, 0.0) - 0.5 * norms

    share = y_lo * RING + x
    own = shift_part(images, shifts.T, share, core, hi)
    own = lax.all_to_all(own, "dom", 0, 0, axis_index_groups=Z_GROUPS)

    send = lambda block, perm: lax.ppermute(block, "orient", perm)
    behind = send(own, AHEAD)
    front = send(own, BACK)
    across = send(own, Y_LOW)
    after, _ = lax.optimization_barrier((front, behind))
    far = send(after, BACK)
    across_front = send(front, Y_LOW)
    across_behind = send(across, AHEAD)
    across_far = send(across_front, BACK)
    ahead = 1 - 2 * core
    here, there = y_lo * RING, (1 - y_lo) * RING
    step = lambda by: (x + by * ahead) % RING
    place = lambda *shares: jnp.stack(shares).astype(jnp.int32)
    parts = (slices, s_hi, s_core, s_both)
    partial, keep, give = add_score(
        place(share, here + step(-1), here + step(1), there + x), (own, behind, front, across), parts, bias[None, :], ()
    )
    partial, keep, give = add_score(
        place(here + step(2), there + step(1), there + step(-1)), (far, across_front, across_behind), parts, partial, (keep, give)
    )
    partial, keep, give = add_score(place(there + step(2)), (across_far,), parts, partial, (keep, give))

    from_hi = lax.ppermute(give, "dom", Y_HIGH)
    from_core = lax.ppermute(keep, "orient", CORE)
    pieces = lax.all_to_all(partial.reshape(HALF, rows, 2 * oris), "dom", 0, 0, axis_index_groups=Z_GROUPS)
    near, other, stats = total_score(pieces)
    came = lax.ppermute(other, "orient", CORE)
    stats = lax.all_to_all(stats, "orient", 0, 0)
    from_hi, stats, came = lax.optimization_barrier((from_hi, stats, came))
    from_both = lax.ppermute(from_hi, "orient", CORE)
    weights, log_norm = weigh(core.astype(jnp.int32)[None], near, came, stats)
    weights = jnp.concatenate([weights, lax.ppermute(weights, "dom", Y_HIGH)])

    around = lambda by, block: lax.ppermute(block, ("orient", "dom"), along_z(by))
    one, back_one = around(1, weights), around(-1, weights)
    two, back_two = around(2, weights), around(-2, weights)
    three, back_three = around(2, one), around(-2, back_one)
    four = around(2, two)
    weights = (weights, one, two, three, four, back_three, back_two, back_one)
    projected = project(place(z, ahead), weights, stage(keep, from_core, from_hi, from_both))
    return projected, log_norm[:, :rows].reshape(2 * rows)


def solution(mesh):
    placed = (P("dom", None), P("dom", None), P("orient", "dom"), P("orient"), P())
    return jax.shard_map(
        on_device,
        mesh=mesh,
        in_specs=placed,
        out_specs=(P("orient", "dom"), P("dom")),
        check_vma=False,
    )
```

```python
import functools
import math

import jax
import jax.numpy as jnp
from jax import lax
from jax.experimental import pallas as pl
from jax.experimental.pallas import tpu as pltpu
from jax.sharding import PartitionSpec as P

BOX = 256
LANES = 128
WIDE = 256
MIB = 1 << 20

ORI = 16
DOM = 16
RING = 4
HALF = DOM // 2
Z_GROUPS = [list(range(HALF)), list(range(HALF, DOM))]
CORE = [(i, i ^ 1) for i in range(ORI)]
Y_LOW = [(i, i ^ 8) for i in range(ORI)]
Y_HIGH = [(i, i ^ 8) for i in range(DOM)]


def along_x(by):
    return [(i, i // 8 * 8 + (i // 2 + by * (1 - i % 2 * 2)) % RING * 2 + i % 2) for i in range(ORI)]


def along_z(by):
    pairs = []
    for o in range(ORI):
        for d in range(DOM):
            z = (d % HALF + by * (1 - o % 2 * 2)) % HALF
            pairs.append((o * DOM + d, o * DOM + d // HALF * HALF + z))
    return pairs


AHEAD = along_x(1)
BACK = along_x(-1)


def turn_wave(turn):
    quarter = (turn + BOX // 8) >> 6
    angle = (turn - (quarter << 6)).astype(jnp.float32) * (2.0 * math.pi / BOX)
    sq = angle * angle
    sine = angle * (1.0 + sq * (-1.0 / 6 + sq * (1.0 / 120 + sq * (-1.0 / 5040 + sq * (1.0 / 362880)))))
    cosine = 1.0 + sq * (-0.5 + sq * (1.0 / 24 + sq * (-1.0 / 720 + sq * (1.0 / 40320))))
    odd = (quarter & 1) == 1
    first = jnp.where(odd, sine, cosine)
    second = jnp.where(odd, cosine, sine)
    first = jnp.where(((quarter + 1) & 2) == 2, -first, first)
    second = jnp.where((quarter & 2) == 2, -second, second)
    return first, second


def shift_kernel(place, shifts, images, out, held, sems):
    share, core, hi = place[0], place[1], place[3]
    zs, _, rows, wide = out.shape
    shares = images.shape[1] // (2 * zs * wide)
    row = pl.ds(pl.multiple_of(core * rows, 16), rows)
    copies = []
    for at in range(2 * zs):
        column = pl.ds(pl.multiple_of((at * shares + share) * wide, wide), wide)
        copies.append(pltpu.make_async_copy(images.at[row, column], held.at[at], sems.at[at]))
        copies[at].start()

    total = shifts.shape[1]
    lane = lax.broadcasted_iota(jnp.int32, (rows, LANES), 1)
    image = lax.broadcasted_iota(jnp.int32, (rows, total), 0) + core * rows
    own = image == lax.broadcasted_iota(jnp.int32, (rows, total), 1)
    by_x = jnp.sum(jnp.where(own, shifts[0:1, :], 0), axis=1, keepdims=True)
    by_y = jnp.sum(jnp.where(own, shifts[1:2, :], 0), axis=1, keepdims=True)
    freq_y = (lane // 2) * (2 * shares) + lane % 2 + 2 * share - place[2]
    cx, sx = turn_wave((lane * by_x) & (BOX - 1))
    cos_y, sin_y = turn_wave((freq_y * by_y) & (BOX - 1))
    for z in range(zs):
        copies[z].wait()
        copies[z + zs].wait()
        for part in range(2):
            pick = 2 * z + part
            cy = cos_y[:, pick : pick + 1]
            sy = sin_y[:, pick : pick + 1]
            cosine = cx * cy - sx * sy
            sine = sx * cy + cx * sy
            here = slice(part * LANES, (part + 1) * LANES)
            re = held[z, :, here].astype(jnp.float32)
            im = held[z + zs, :, here].astype(jnp.float32)
            out[z, hi, :, here] = (re * cosine + im * sine).astype(jnp.bfloat16)
            out[z, 1 - hi, :, here] = (im * cosine - re * sine).astype(jnp.bfloat16)


def shift_part(images, shifts, share, core, hi):
    rows, width = images.shape
    rows = rows // 2
    place = jnp.stack([share, core, jnp.int32(width // 2 // 256), hi]).astype(jnp.int32)
    vmem = pl.BlockSpec(memory_space=pltpu.VMEM)
    return pl.pallas_call(
        shift_kernel,
        out_shape=jax.ShapeDtypeStruct((HALF, 2, rows, WIDE), jnp.bfloat16),
        in_specs=[pl.BlockSpec(memory_space=pltpu.SMEM), vmem, pl.BlockSpec(memory_space=pl.ANY)],
        out_specs=vmem,
        scratch_shapes=[pltpu.VMEM((DOM, rows, WIDE), jnp.bfloat16), pltpu.SemaphoreType.DMA((DOM,))],
        compiler_params=pltpu.CompilerParams(vmem_limit_bytes=60 * MIB),
        name="shift",
    )(place, shifts, images)


def score_kernel(count, place, *refs):
    blocks, refs = refs[:count], refs[count:]
    slices, refs = refs[: 4 * count], refs[4 * count :]
    before, out, keep, give, sems = refs[0], *refs[-4:]
    images, oris = out.shape
    wide = blocks[0].shape[-1]
    copies = []
    for k, block in enumerate(blocks):
        for side, filed in enumerate((keep, give)):
            copies.append(pltpu.make_async_copy(block.at[:, side], filed.at[place[k]], sems.at[2 * k + side]))
    for copy in copies:
        copy.start()
    dims = (((1,), (1,)), ((), ()))
    left = jnp.concatenate([block[:, side].reshape(images, wide) for side in range(2) for block in blocks], axis=1)
    for at in range(2):
        right = jnp.concatenate([slices[(2 * at + side) * count + k][...] for side in range(2) for k in range(count)], axis=1)
        here = slice(at * oris // 2, (at + 1) * oris // 2)
        out[:, here] = lax.dot_general(left, right, dims, preferred_element_type=jnp.float32) + before[:, here]
    for copy in copies:
        copy.wait()


def add_score(place, blocks, slices, before, filed):
    count = len(blocks)
    zs, _, rows, wide = blocks[0].shape
    oris, width = slices[0].shape
    shares = width // wide
    images = zs * rows
    every = lambda shape: pl.BlockSpec(shape, lambda i, place: (0,) * len(shape))
    chunk = lambda k: pl.BlockSpec((oris, wide), lambda i, place: (0, place[k]))
    anywhere = pl.BlockSpec(memory_space=pl.ANY)
    whole = pltpu.HBM((shares, zs, rows, wide), jnp.bfloat16)
    total = (pltpu.HBM if count == 1 else jax.ShapeDtypeStruct)((images, 2 * oris), jnp.float32)
    inputs = [*blocks, *(part for part in slices for _ in range(count)), before, *filed]
    return pl.pallas_call(
        functools.partial(score_kernel, count),
        out_shape=(total, whole, whole),
        grid_spec=pltpu.PrefetchScalarGridSpec(
            num_scalar_prefetch=1,
            grid=(1,),
            in_specs=[every(block.shape) for block in blocks]
            + [chunk(k) for _ in slices for k in range(count)]
            + [every(before.shape)]
            + [anywhere] * len(filed),
            out_specs=[every((images, 2 * oris)), anywhere, anywhere],
            scratch_shapes=[pltpu.SemaphoreType.DMA((2 * count,))],
        ),
        input_output_aliases={len(inputs) - 1: 1, len(inputs): 2} if filed else {},
        compiler_params=pltpu.CompilerParams(vmem_limit_bytes=24 * MIB),
        name="score",
    )(place, *inputs)


def to_row(column):
    rows = column.shape[0]
    wide = jnp.broadcast_to(column, (rows, LANES))
    square = jnp.concatenate([wide, jnp.zeros((LANES - rows, LANES), jnp.float32)], axis=0)
    return jnp.transpose(square)[0:1]


def to_column(row, rows):
    return jnp.transpose(jnp.broadcast_to(row, (LANES, LANES)))[:rows, 0:1]


def total_kernel(pieces, near, other, stats):
    total = pieces[0]
    for d in range(1, pieces.shape[0]):
        total = total + pieces[d]
    oris = near.shape[1]
    near[...] = total[:, :oris]
    other[...] = total[:, oris:]
    peak = jnp.max(total, axis=1, keepdims=True)
    mass = jnp.sum(jnp.exp(total - peak), axis=1, keepdims=True)
    both = jnp.concatenate([to_row(peak), to_row(mass), jnp.zeros((6, LANES), jnp.float32)], axis=0)
    stats[...] = jnp.broadcast_to(both[None], stats.shape)


def total_score(pieces):
    _, rows, oris = pieces.shape
    return pl.pallas_call(
        total_kernel,
        out_shape=(
            jax.ShapeDtypeStruct((rows, oris // 2), jnp.float32),
            jax.ShapeDtypeStruct((rows, oris // 2), jnp.float32),
            jax.ShapeDtypeStruct((ORI, 8, LANES), jnp.float32),
        ),
        compiler_params=pltpu.CompilerParams(vmem_limit_bytes=32 * MIB),
        name="total",
    )(pieces)


def weight_kernel(place, near, came, stats, weights, log_norm):
    rows = near.shape[0]
    core = place[0]
    used = lax.broadcasted_iota(jnp.int32, (1, LANES), 1) < rows
    peak, total = [], []
    for c in range(2):
        peaks = jnp.concatenate([stats[p, 0:1, :] for p in range(c, ORI, 2)], axis=0)
        masses = jnp.concatenate([stats[p, 1:2, :] for p in range(c, ORI, 2)], axis=0)
        top = jnp.max(peaks, axis=0, keepdims=True)
        mass = jnp.sum(masses * jnp.exp(peaks - top), axis=0, keepdims=True)
        peak.append(top)
        total.append(jnp.where(used, mass, 1.0))
        log_norm[c : c + 1, :] = top + jnp.log(total[c])
    for at, (c, part) in enumerate(((core, near), (1 - core, came))):
        top = to_column(jnp.where(c == 0, peak[0], peak[1]), rows)
        mass = to_column(jnp.where(c == 0, total[0], total[1]), rows)
        weights[at] = (jnp.exp(part[...] - top) / mass).astype(jnp.bfloat16)


def weigh(place, near, came, stats):
    rows, oris = near.shape
    vmem = pl.BlockSpec(memory_space=pltpu.VMEM)
    return pl.pallas_call(
        weight_kernel,
        out_shape=(
            jax.ShapeDtypeStruct((2, rows, oris), jnp.bfloat16),
            jax.ShapeDtypeStruct((2, LANES), jnp.float32),
        ),
        in_specs=[pl.BlockSpec(memory_space=pltpu.SMEM), vmem, vmem, vmem],
        out_specs=(vmem, vmem),
        compiler_params=pltpu.CompilerParams(vmem_limit_bytes=16 * MIB),
        name="weigh",
    )(place, near, came, stats)


def stage_kernel(*refs):
    columns, out, sems = refs[:-2], refs[-2], refs[-1]
    copies = [pltpu.make_async_copy(column, out.at[g], sems.at[g]) for g, column in enumerate(columns)]
    for copy in copies:
        copy.start()
    for copy in copies:
        copy.wait()


def stage(*columns):
    anywhere = pl.BlockSpec(memory_space=pl.ANY)
    return pl.pallas_call(
        stage_kernel,
        out_shape=pltpu.VMEM((len(columns), *columns[0].shape), jnp.bfloat16),
        in_specs=[anywhere] * len(columns),
        out_specs=anywhere,
        scratch_shapes=[pltpu.SemaphoreType.DMA((len(columns),))],
        compiler_params=pltpu.CompilerParams(vmem_limit_bytes=16 * MIB),
        cost_estimate=pl.CostEstimate(flops=0, transcendentals=0, bytes_accessed=12 * MIB),
        name="stage",
    )(*columns)


def project_kernel(place, *refs):
    zs = HALF
    weights, columns, (out, left, done, sems) = refs[:zs], refs[zs], refs[zs + 1 :]
    groups, rows, oris = weights[0].shape
    images = zs * rows
    _, shares, _, _, wide = columns.shape
    for k, block in enumerate(weights):
        z = lax.rem(place[0] + zs - k * place[1], zs)
        for g in range(groups):
            left[pl.ds(pl.multiple_of(g * images + z * rows, 16), rows), :] = block[g]
    copies = []
    for at in range(0, shares, 2):
        right = jnp.concatenate(
            [columns[:, s].reshape(groups * images, wide) for s in (at, at + 1)], axis=1
        )
        done[at // 2] = lax.dot_general(left[...], right, (((0,), (0,)), ((), ())), preferred_element_type=jnp.float32)
        here = pl.ds(at * wide, 2 * wide)
        copies.append(pltpu.make_async_copy(done.at[at // 2], out.at[:, here], sems.at[at // 2]))
        copies[-1].start()
    for copy in copies:
        copy.wait()


def project(place, weights, columns):
    _, shares, zs, rows, wide = columns.shape
    groups, _, oris = weights[0].shape
    vmem = pl.BlockSpec(memory_space=pltpu.VMEM)
    return pl.pallas_call(
        project_kernel,
        out_shape=jax.ShapeDtypeStruct((oris, shares * wide), jnp.float32),
        in_specs=[pl.BlockSpec(memory_space=pltpu.SMEM)] + [vmem] * (len(weights) + 1),
        out_specs=pl.BlockSpec(memory_space=pl.ANY),
        scratch_shapes=[
            pltpu.VMEM((groups * zs * rows, oris), jnp.bfloat16),
            pltpu.VMEM((shares // 2, oris, 2 * wide), jnp.float32),
            pltpu.SemaphoreType.DMA((shares // 2,)),
        ],
        compiler_params=pltpu.CompilerParams(vmem_limit_bytes=32 * MIB),
        name="project",
    )(place, *weights, columns)


def squares(block):
    block = block.astype(jnp.float32)
    return jnp.sum(block * block, axis=1)


def on_device(images, shifts, slices, class_of, log_prior):
    rows = images.shape[0] // 2
    oris = slices.shape[0]
    orient = lax.axis_index("orient")
    dom = lax.axis_index("dom")
    core, x, y_lo = orient % 2, orient // 2 % RING, orient // 8
    hi, z = dom // HALF, dom % HALF

    s_hi = lax.ppermute(slices, "dom", Y_HIGH)
    s_core = lax.ppermute(slices, "orient", CORE)
    s_both = lax.ppermute(s_hi, "orient", CORE)
    onehot = class_of[:, None] == jnp.arange(log_prior.shape[0], dtype=jnp.int32)[None, :]
    prior = jnp.sum(jnp.where(onehot, log_prior[None, :], 0.0), axis=1)
    prior = jnp.concatenate([prior, lax.ppermute(prior, "orient", CORE)])
    norms = jnp.concatenate([squares(slices) + squares(s_hi), squares(s_core) + squares(s_both)])
    bias = jnp.where(z == 0, prior, 0.0) - 0.5 * norms

    share = y_lo * RING + x
    own = shift_part(images, shifts.T, share, core, hi)
    own = lax.all_to_all(own, "dom", 0, 0, axis_index_groups=Z_GROUPS)

    send = lambda block, perm: lax.ppermute(block, "orient", perm)
    behind = send(own, AHEAD)
    front = send(own, BACK)
    across = send(own, Y_LOW)
    far = send(front, BACK)
    across_front = send(front, Y_LOW)
    across_behind = send(across, AHEAD)
    across_far = send(across_front, BACK)
    ahead = 1 - 2 * core
    here, there = y_lo * RING, (1 - y_lo) * RING
    step = lambda by: (x + by * ahead) % RING
    place = lambda *shares: jnp.stack(shares).astype(jnp.int32)
    parts = (slices, s_hi, s_core, s_both)
    partial, keep, give = add_score(
        place(share, here + step(-1), here + step(1), there + x), (own, behind, front, across), parts, bias[None, :], ()
    )
    partial, keep, give = add_score(
        place(here + step(2), there + step(1), there + step(-1)), (far, across_front, across_behind), parts, partial, (keep, give)
    )
    partial, keep, give = add_score(place(there + step(2)), (across_far,), parts, partial, (keep, give))

    from_hi = lax.ppermute(give, "dom", Y_HIGH)
    from_core = lax.ppermute(keep, "orient", CORE)
    pieces = lax.all_to_all(partial.reshape(HALF, rows, 2 * oris), "dom", 0, 0, axis_index_groups=Z_GROUPS)
    near, other, stats = total_score(pieces)
    came = lax.ppermute(other, "orient", CORE)
    stats = lax.all_to_all(stats, "orient", 0, 0)
    from_hi, stats, came = lax.optimization_barrier((from_hi, stats, came))
    from_both = lax.ppermute(from_hi, "orient", CORE)
    weights, log_norm = weigh(core.astype(jnp.int32)[None], near, came, stats)
    weights = jnp.concatenate([weights, lax.ppermute(weights, "dom", Y_HIGH)])

    around = lambda by, block: lax.ppermute(block, ("orient", "dom"), along_z(by))
    one, back_one = around(1, weights), around(-1, weights)
    two, back_two = around(2, weights), around(-2, weights)
    three, back_three = around(2, one), around(-2, back_one)
    four = around(2, two)
    weights = (weights, one, two, three, four, back_three, back_two, back_one)
    projected = project(place(z, ahead), weights, stage(keep, from_core, from_hi, from_both))
    return projected, log_norm[:, :rows].reshape(2 * rows)


def solution(mesh):
    placed = (P("dom", None), P("dom", None), P("orient", "dom"), P("orient"), P())
    return jax.shard_map(
        on_device,
        mesh=mesh,
        in_specs=placed,
        out_specs=(P("orient", "dom"), P("dom")),
        check_vma=False,
    )
```

```python
import functools
import math

import jax
import jax.numpy as jnp
from jax import lax
from jax.experimental import pallas as pl
from jax.experimental.pallas import tpu as pltpu
from jax.sharding import PartitionSpec as P

BOX = 256
LANES = 128
WIDE = 256
MIB = 1 << 20

ORI = 16
DOM = 16
RING = 4
HALF = DOM // 2
Z_GROUPS = [list(range(HALF)), list(range(HALF, DOM))]
CORE = [(i, i ^ 1) for i in range(ORI)]
Y_LOW = [(i, i ^ 8) for i in range(ORI)]
Y_HIGH = [(i, i ^ 8) for i in range(DOM)]


def along_x(by):
    return [(i, i // 8 * 8 + (i // 2 + by * (1 - i % 2 * 2)) % RING * 2 + i % 2) for i in range(ORI)]


def along_z(by):
    pairs = []
    for o in range(ORI):
        for d in range(DOM):
            z = (d % HALF + by * (1 - o % 2 * 2)) % HALF
            pairs.append((o * DOM + d, o * DOM + d // HALF * HALF + z))
    return pairs


AHEAD = along_x(1)
BACK = along_x(-1)


def turn_wave(turn):
    quarter = (turn + BOX // 8) >> 6
    angle = (turn - (quarter << 6)).astype(jnp.float32) * (2.0 * math.pi / BOX)
    sq = angle * angle
    sine = angle * (1.0 + sq * (-1.0 / 6 + sq * (1.0 / 120 + sq * (-1.0 / 5040 + sq * (1.0 / 362880)))))
    cosine = 1.0 + sq * (-0.5 + sq * (1.0 / 24 + sq * (-1.0 / 720 + sq * (1.0 / 40320))))
    odd = (quarter & 1) == 1
    first = jnp.where(odd, sine, cosine)
    second = jnp.where(odd, cosine, sine)
    first = jnp.where(((quarter + 1) & 2) == 2, -first, first)
    second = jnp.where((quarter & 2) == 2, -second, second)
    return first, second


def shift_kernel(place, shifts, images, out, held, sems):
    share, core, hi = place[0], place[1], place[3]
    zs, _, rows, wide = out.shape
    shares = images.shape[1] // (2 * zs * wide)
    row = pl.ds(pl.multiple_of(core * rows, 16), rows)
    copies = []
    for at in range(2 * zs):
        column = pl.ds(pl.multiple_of((at * shares + share) * wide, wide), wide)
        copies.append(pltpu.make_async_copy(images.at[row, column], held.at[at], sems.at[at]))
        copies[at].start()

    total = shifts.shape[1]
    lane = lax.broadcasted_iota(jnp.int32, (rows, LANES), 1)
    image = lax.broadcasted_iota(jnp.int32, (rows, total), 0) + core * rows
    own = image == lax.broadcasted_iota(jnp.int32, (rows, total), 1)
    by_x = jnp.sum(jnp.where(own, shifts[0:1, :], 0), axis=1, keepdims=True)
    by_y = jnp.sum(jnp.where(own, shifts[1:2, :], 0), axis=1, keepdims=True)
    freq_y = (lane // 2) * (2 * shares) + lane % 2 + 2 * share - place[2]
    cx, sx = turn_wave((lane * by_x) & (BOX - 1))
    cos_y, sin_y = turn_wave((freq_y * by_y) & (BOX - 1))
    for z in range(zs):
        copies[z].wait()
        copies[z + zs].wait()
        for part in range(2):
            pick = 2 * z + part
            cy = cos_y[:, pick : pick + 1]
            sy = sin_y[:, pick : pick + 1]
            cosine = cx * cy - sx * sy
            sine = sx * cy + cx * sy
            here = slice(part * LANES, (part + 1) * LANES)
            re = held[z, :, here].astype(jnp.float32)
            im = held[z + zs, :, here].astype(jnp.float32)
            out[z, hi, :, here] = (re * cosine + im * sine).astype(jnp.bfloat16)
            out[z, 1 - hi, :, here] = (im * cosine - re * sine).astype(jnp.bfloat16)


def shift_part(images, shifts, share, core, hi):
    rows, width = images.shape
    rows = rows // 2
    place = jnp.stack([share, core, jnp.int32(width // 2 // 256), hi]).astype(jnp.int32)
    vmem = pl.BlockSpec(memory_space=pltpu.VMEM)
    return pl.pallas_call(
        shift_kernel,
        out_shape=jax.ShapeDtypeStruct((HALF, 2, rows, WIDE), jnp.bfloat16),
        in_specs=[pl.BlockSpec(memory_space=pltpu.SMEM), vmem, pl.BlockSpec(memory_space=pl.ANY)],
        out_specs=vmem,
        scratch_shapes=[pltpu.VMEM((DOM, rows, WIDE), jnp.bfloat16), pltpu.SemaphoreType.DMA((DOM,))],
        compiler_params=pltpu.CompilerParams(vmem_limit_bytes=60 * MIB),
        name="shift",
    )(place, shifts, images)


def score_kernel(count, place, *refs):
    blocks, refs = refs[:count], refs[count:]
    slices, refs = refs[: 4 * count], refs[4 * count :]
    before, out, keep, give, sems = refs[0], *refs[-4:]
    images, oris = out.shape
    wide = blocks[0].shape[-1]
    copies = []
    for k, block in enumerate(blocks):
        for side, filed in enumerate((keep, give)):
            copies.append(pltpu.make_async_copy(block.at[:, side], filed.at[place[k]], sems.at[2 * k + side]))
    for copy in copies:
        copy.start()
    dims = (((1,), (1,)), ((), ()))
    left = jnp.concatenate([block[:, side].reshape(images, wide) for side in range(2) for block in blocks], axis=1)
    for at in range(2):
        right = jnp.concatenate([slices[(2 * at + side) * count + k][...] for side in range(2) for k in range(count)], axis=1)
        here = slice(at * oris // 2, (at + 1) * oris // 2)
        out[:, here] = lax.dot_general(left, right, dims, preferred_element_type=jnp.float32) + before[:, here]
    for copy in copies:
        copy.wait()


def add_score(place, blocks, slices, before, filed):
    count = len(blocks)
    zs, _, rows, wide = blocks[0].shape
    oris, width = slices[0].shape
    shares = width // wide
    images = zs * rows
    every = lambda shape: pl.BlockSpec(shape, lambda i, place: (0,) * len(shape))
    chunk = lambda k: pl.BlockSpec((oris, wide), lambda i, place: (0, place[k]))
    anywhere = pl.BlockSpec(memory_space=pl.ANY)
    whole = pltpu.HBM((shares, zs, rows, wide), jnp.bfloat16)
    total = (pltpu.HBM if count == 1 else jax.ShapeDtypeStruct)((images, 2 * oris), jnp.float32)
    inputs = [*blocks, *(part for part in slices for _ in range(count)), before, *filed]
    return pl.pallas_call(
        functools.partial(score_kernel, count),
        out_shape=(total, whole, whole),
        grid_spec=pltpu.PrefetchScalarGridSpec(
            num_scalar_prefetch=1,
            grid=(1,),
            in_specs=[every(block.shape) for block in blocks]
            + [chunk(k) for _ in slices for k in range(count)]
            + [every(before.shape)]
            + [anywhere] * len(filed),
            out_specs=[every((images, 2 * oris)), anywhere, anywhere],
            scratch_shapes=[pltpu.SemaphoreType.DMA((2 * count,))],
        ),
        input_output_aliases={len(inputs) - 1: 1, len(inputs): 2} if filed else {},
        compiler_params=pltpu.CompilerParams(vmem_limit_bytes=24 * MIB),
        name="score",
    )(place, *inputs)


def to_row(column):
    rows = column.shape[0]
    wide = jnp.broadcast_to(column, (rows, LANES))
    square = jnp.concatenate([wide, jnp.zeros((LANES - rows, LANES), jnp.float32)], axis=0)
    return jnp.transpose(square)[0:1]


def to_column(row, rows):
    return jnp.transpose(jnp.broadcast_to(row, (LANES, LANES)))[:rows, 0:1]


def total_kernel(pieces, near, other, stats):
    total = pieces[0]
    for d in range(1, pieces.shape[0]):
        total = total + pieces[d]
    oris = near.shape[1]
    near[...] = total[:, :oris]
    other[...] = total[:, oris:]
    peak = jnp.max(total, axis=1, keepdims=True)
    mass = jnp.sum(jnp.exp(total - peak), axis=1, keepdims=True)
    both = jnp.concatenate([to_row(peak), to_row(mass), jnp.zeros((6, LANES), jnp.float32)], axis=0)
    stats[...] = jnp.broadcast_to(both[None], stats.shape)


def total_score(pieces):
    _, rows, oris = pieces.shape
    return pl.pallas_call(
        total_kernel,
        out_shape=(
            jax.ShapeDtypeStruct((rows, oris // 2), jnp.float32),
            jax.ShapeDtypeStruct((rows, oris // 2), jnp.float32),
            jax.ShapeDtypeStruct((ORI, 8, LANES), jnp.float32),
        ),
        compiler_params=pltpu.CompilerParams(vmem_limit_bytes=32 * MIB),
        name="total",
    )(pieces)


def weight_kernel(place, near, came, stats, weights, log_norm):
    rows = near.shape[0]
    core = place[0]
    used = lax.broadcasted_iota(jnp.int32, (1, LANES), 1) < rows
    peak, total = [], []
    for c in range(2):
        peaks = jnp.concatenate([stats[p, 0:1, :] for p in range(c, ORI, 2)], axis=0)
        masses = jnp.concatenate([stats[p, 1:2, :] for p in range(c, ORI, 2)], axis=0)
        top = jnp.max(peaks, axis=0, keepdims=True)
        mass = jnp.sum(masses * jnp.exp(peaks - top), axis=0, keepdims=True)
        peak.append(top)
        total.append(jnp.where(used, mass, 1.0))
        log_norm[c : c + 1, :] = top + jnp.log(total[c])
    for at, (c, part) in enumerate(((core, near), (1 - core, came))):
        top = to_column(jnp.where(c == 0, peak[0], peak[1]), rows)
        mass = to_column(jnp.where(c == 0, total[0], total[1]), rows)
        weights[at] = (jnp.exp(part[...] - top) / mass).astype(jnp.bfloat16)


def weigh(place, near, came, stats):
    rows, oris = near.shape
    vmem = pl.BlockSpec(memory_space=pltpu.VMEM)
    return pl.pallas_call(
        weight_kernel,
        out_shape=(
            jax.ShapeDtypeStruct((2, rows, oris), jnp.bfloat16),
            jax.ShapeDtypeStruct((2, LANES), jnp.float32),
        ),
        in_specs=[pl.BlockSpec(memory_space=pltpu.SMEM), vmem, vmem, vmem],
        out_specs=(vmem, vmem),
        compiler_params=pltpu.CompilerParams(vmem_limit_bytes=16 * MIB),
        name="weigh",
    )(place, near, came, stats)


def stage_kernel(*refs):
    columns, out, sems = refs[:-2], refs[-2], refs[-1]
    copies = [pltpu.make_async_copy(column, out.at[g], sems.at[g]) for g, column in enumerate(columns)]
    for copy in copies:
        copy.start()
    for copy in copies:
        copy.wait()


def stage(*columns):
    anywhere = pl.BlockSpec(memory_space=pl.ANY)
    return pl.pallas_call(
        stage_kernel,
        out_shape=pltpu.VMEM((len(columns), *columns[0].shape), jnp.bfloat16),
        in_specs=[anywhere] * len(columns),
        out_specs=anywhere,
        scratch_shapes=[pltpu.SemaphoreType.DMA((len(columns),))],
        compiler_params=pltpu.CompilerParams(vmem_limit_bytes=16 * MIB),
        cost_estimate=pl.CostEstimate(flops=0, transcendentals=0, bytes_accessed=12 * MIB),
        name="stage",
    )(*columns)


def project_kernel(place, *refs):
    zs = HALF
    weights, columns, (out, left, done, sems) = refs[:zs], refs[zs], refs[zs + 1 :]
    groups, rows, oris = weights[0].shape
    images = zs * rows
    _, shares, _, _, wide = columns.shape
    for k, block in enumerate(weights):
        z = lax.rem(place[0] + zs - k * place[1], zs)
        for g in range(groups):
            left[pl.ds(pl.multiple_of(g * images + z * rows, 16), rows), :] = block[g]
    copies = []
    for at in range(0, shares, 2):
        right = jnp.concatenate(
            [columns[:, s].reshape(groups * images, wide) for s in (at, at + 1)], axis=1
        )
        done[at // 2] = lax.dot_general(left[...], right, (((0,), (0,)), ((), ())), preferred_element_type=jnp.float32)
        here = pl.ds(at * wide, 2 * wide)
        copies.append(pltpu.make_async_copy(done.at[at // 2], out.at[:, here], sems.at[at // 2]))
        copies[-1].start()
    for copy in copies:
        copy.wait()


def project(place, weights, columns):
    _, shares, zs, rows, wide = columns.shape
    groups, _, oris = weights[0].shape
    vmem = pl.BlockSpec(memory_space=pltpu.VMEM)
    return pl.pallas_call(
        project_kernel,
        out_shape=jax.ShapeDtypeStruct((oris, shares * wide), jnp.float32),
        in_specs=[pl.BlockSpec(memory_space=pltpu.SMEM)] + [vmem] * (len(weights) + 1),
        out_specs=pl.BlockSpec(memory_space=pl.ANY),
        scratch_shapes=[
            pltpu.VMEM((groups * zs * rows, oris), jnp.bfloat16),
            pltpu.VMEM((shares // 2, oris, 2 * wide), jnp.float32),
            pltpu.SemaphoreType.DMA((shares // 2,)),
        ],
        compiler_params=pltpu.CompilerParams(vmem_limit_bytes=32 * MIB),
        name="project",
    )(place, *weights, columns)


def squares(block):
    block = block.astype(jnp.float32)
    return jnp.sum(block * block, axis=1)


def on_device(images, shifts, slices, class_of, log_prior):
    rows = images.shape[0] // 2
    oris = slices.shape[0]
    orient = lax.axis_index("orient")
    dom = lax.axis_index("dom")
    core, x, y_lo = orient % 2, orient // 2 % RING, orient // 8
    hi, z = dom // HALF, dom % HALF

    s_hi = lax.ppermute(slices, "dom", Y_HIGH)
    s_core = lax.ppermute(slices, "orient", CORE)
    share = y_lo * RING + x
    own = shift_part(images, shifts.T, share, core, hi)
    own = lax.all_to_all(own, "dom", 0, 0, axis_index_groups=Z_GROUPS)

    s_hi, _ = lax.optimization_barrier((s_hi, own))
    s_both = lax.ppermute(s_hi, "orient", CORE)
    onehot = class_of[:, None] == jnp.arange(log_prior.shape[0], dtype=jnp.int32)[None, :]
    prior = jnp.sum(jnp.where(onehot, log_prior[None, :], 0.0), axis=1)
    prior = jnp.concatenate([prior, lax.ppermute(prior, "orient", CORE)])
    norms = jnp.concatenate([squares(slices) + squares(s_hi), squares(s_core) + squares(s_both)])
    bias = jnp.where(z == 0, prior, 0.0) - 0.5 * norms

    send = lambda block, perm: lax.ppermute(block, "orient", perm)
    behind = send(own, AHEAD)
    front = send(own, BACK)
    across = send(own, Y_LOW)
    far = send(front, BACK)
    across_front = send(front, Y_LOW)
    across_behind = send(across, AHEAD)
    across_far = send(across_front, BACK)
    ahead = 1 - 2 * core
    here, there = y_lo * RING, (1 - y_lo) * RING
    step = lambda by: (x + by * ahead) % RING
    place = lambda *shares: jnp.stack(shares).astype(jnp.int32)
    parts = (slices, s_hi, s_core, s_both)
    partial, keep, give = add_score(
        place(share, here + step(-1), here + step(1), there + x), (own, behind, front, across), parts, bias[None, :], ()
    )
    partial, keep, give = add_score(
        place(here + step(2), there + step(1), there + step(-1)), (far, across_front, across_behind), parts, partial, (keep, give)
    )
    partial, keep, give = add_score(place(there + step(2)), (across_far,), parts, partial, (keep, give))

    from_hi = lax.ppermute(give, "dom", Y_HIGH)
    from_core = lax.ppermute(keep, "orient", CORE)
    pieces = lax.all_to_all(partial.reshape(HALF, rows, 2 * oris), "dom", 0, 0, axis_index_groups=Z_GROUPS)
    near, other, stats = total_score(pieces)
    came = lax.ppermute(other, "orient", CORE)
    stats = lax.all_to_all(stats, "orient", 0, 0)
    from_hi, stats, came = lax.optimization_barrier((from_hi, stats, came))
    from_both = lax.ppermute(from_hi, "orient", CORE)
    weights, log_norm = weigh(core.astype(jnp.int32)[None], near, came, stats)
    weights = jnp.concatenate([weights, lax.ppermute(weights, "dom", Y_HIGH)])

    around = lambda by, block: lax.ppermute(block, ("orient", "dom"), along_z(by))
    one, back_one = around(1, weights), around(-1, weights)
    two, back_two = around(2, weights), around(-2, weights)
    three, back_three = around(2, one), around(-2, back_one)
    four = around(2, two)
    weights = (weights, one, two, three, four, back_three, back_two, back_one)
    projected = project(place(z, ahead), weights, stage(keep, from_core, from_hi, from_both))
    return projected, log_norm[:, :rows].reshape(2 * rows)


def solution(mesh):
    placed = (P("dom", None), P("dom", None), P("orient", "dom"), P("orient"), P())
    return jax.shard_map(
        on_device,
        mesh=mesh,
        in_specs=placed,
        out_specs=(P("orient", "dom"), P("dom")),
        check_vma=False,
    )
```
